768 devices in a mesh: dp: 96 (over z, x, y_hi), group: 8 (over y_lo, core).
Axes of the slice: x: 4, y: 8 (y_hi: 2, y_lo: 4; y = y_hi * 4 + y_lo), z: 12, core: 2. Of those that a mesh axis runs over, the one named last changes fastest.
Arguments:
- image: bfloat16 [294912, 1152], P(('dp', 'group')), may hold values from -0.1875 to 0.1875
- text: bfloat16 [294912, 1152], P(('dp', 'group')), may hold values from -0.1875 to 0.1875
- caption_index: int32 [768, 384], P(('dp', 'group')), may hold values from 0 to 383, each once within a row
- log_scale: float32 [], replicated, may hold values from 1.5 to 3
- bias: float32 [], replicated, may hold values from -4 to -1
Outputs:
- grad_image: bfloat16 [294912, 1152], P(('dp', 'group'))
- grad_text: bfloat16 [294912, 1152], P(('dp', 'group'))
- row_loss: float32 [294912], P(('dp', 'group'))
The draws below stay inside these ranges and needn't reach their ends.
Inputs may be any that keep to these rules, and one draw needn't show every extreme that they name: Each row of caption_index holds every number below 384 exactly once.
All inputs are finite; a program needn't handle non-finite values.
Results may differ from the reference program's by a relative error of at most 0.0095.
Values may be sent and summed in bfloat16 or wider, within the bound.
A program may use at most 32 MiB of HBM per device.

```python
import jax
import jax.numpy as jnp
from jax import lax

D = 1152
ROWS = 384
BLOCKS = 768
TOKENS = 294912
SHIFT_FAR = 385
N_GROUP = 8


def level_of(key, extent, shards, low, largest):
    level, own = 1.0, jax.random.fold_in(key, 6)
    for axis_at, blocks in shards:
        heights = jnp.exp(jax.random.uniform(jax.random.fold_in(own, axis_at), (blocks,), jnp.float32, low / len(shards), largest / len(shards)))
        level = level * jnp.repeat(heights, extent[axis_at] // blocks).reshape([-1 if axis == axis_at else 1 for axis in range(len(extent))])
    return level


def normal_values(stream_key, shape, spread, limit, cuts=(), kind=jnp.bfloat16):
    level = level_of(stream_key, shape, cuts, -0.22, 0.18) if cuts else 1.0
    entries = jax.random.normal(stream_key, shape, jnp.float32) * spread * level
    return jnp.minimum(jnp.maximum(entries, -limit), limit).astype(kind)


def setup_inputs(seed: int = 0) -> dict:
    key_list = jax.random.split(jax.random.key(seed), 6)
    return {
        "image": normal_values(key_list[0], (TOKENS, D), D ** -0.5, 0.1875, ((0, 768),)),
        "text": normal_values(key_list[1], (TOKENS, D), D ** -0.5, 0.1875, ((0, 768),)),
        "caption_index": jax.vmap(lambda own: jax.random.permutation(own, ROWS))(jax.random.split(key_list[2], BLOCKS)).reshape((BLOCKS, ROWS)).astype(jnp.int32),
        "log_scale": jnp.clip(jax.random.uniform(key_list[3], (), jnp.float32, 1.5, 3.0), 1.5, 3.0),
        "bias": jnp.clip(jax.random.uniform(key_list[4], (), jnp.float32, -4.0, -1.0), -4.0, -1.0),
    }


def tile_terms(image_rows, text_rows, scale, bias, positive):
    logits = scale * jnp.dot(image_rows, text_rows.T, preferred_element_type=jnp.float32) + bias
    signs = jnp.where(positive, jnp.float32(1.0), jnp.float32(-1.0))
    terms = jax.nn.softplus(-signs * logits)
    coef = (jax.nn.sigmoid(logits) - positive.astype(jnp.float32)).astype(jnp.bfloat16)
    return jnp.sum(terms, axis=1), coef


def reference(image, text, caption_index, log_scale, bias):
    scale = jnp.exp(log_scale)
    columns = jnp.arange(ROWS, dtype=jnp.int32)
    nothing = jnp.zeros((ROWS, ROWS), dtype=bool)

    def block_of(array, index):
        return lax.dynamic_slice_in_dim(array, (index * ROWS).astype(jnp.int32), ROWS, 0)

    def forward(block):
        own_image = block_of(image, block)
        own_text = block_of(text, block)
        near_text = block_of(text, (block - N_GROUP) % BLOCKS)
        far_text = block_of(text, (block - SHIFT_FAR) % BLOCKS)
        positive = caption_index[block][:, None] == columns[None, :]
        loss_own, coef_own = tile_terms(own_image, own_text, scale, bias, positive)
        loss_near, coef_near = tile_terms(own_image, near_text, scale, bias, nothing)
        loss_far, coef_far = tile_terms(own_image, far_text, scale, bias, nothing)
        image_near = (scale * jnp.dot(coef_near, near_text, preferred_element_type=jnp.float32)).astype(jnp.bfloat16)
        image_far = (scale * jnp.dot(coef_far, far_text, preferred_element_type=jnp.float32)).astype(jnp.bfloat16)
        grad_rows = scale * jnp.dot(coef_own, own_text, preferred_element_type=jnp.float32)
        grad_rows = (grad_rows + image_near.astype(jnp.float32) + image_far.astype(jnp.float32)).astype(jnp.bfloat16)
        text_near = (scale * jnp.dot(coef_near.T, own_image, preferred_element_type=jnp.float32)).astype(jnp.bfloat16)
        text_far = (scale * jnp.dot(coef_far.T, own_image, preferred_element_type=jnp.float32)).astype(jnp.bfloat16)
        losses = (loss_own + loss_near + loss_far) / jnp.float32(3 * ROWS)
        return grad_rows, losses, text_near, text_far

    indices = jnp.arange(BLOCKS, dtype=jnp.int32)
    grad_image, row_loss, parts_near, parts_far = lax.map(forward, indices)

    def backward(block):
        own_image = block_of(image, block)
        own_text = block_of(text, block)
        positive = caption_index[block][:, None] == columns[None, :]
        unused, coef_own = tile_terms(own_image, own_text, scale, bias, positive)
        total = scale * jnp.dot(coef_own.T, own_image, preferred_element_type=jnp.float32)
        total = total + parts_near[(block + N_GROUP) % BLOCKS].astype(jnp.float32)
        total = total + parts_far[(block + SHIFT_FAR) % BLOCKS].astype(jnp.float32)
        return total.astype(jnp.bfloat16)

    grad_text = lax.map(backward, indices)
    return grad_image.reshape(TOKENS, D), grad_text.reshape(TOKENS, D), row_loss.reshape(TOKENS)
```

```python
import functools

import jax
import jax.numpy as jnp
from jax import lax
from jax.experimental import pallas as pl
from jax.experimental.pallas import tpu as pltpu
from jax.sharding import PartitionSpec as P

MESH = pl.DeviceIdType.MESH
CHUNKS = 4


def dot_nt(a, b):
    return lax.dot_general(a, b, (((1,), (1,)), ((), ())), preferred_element_type=jnp.float32)


def dot_tn(a, b):
    return lax.dot_general(a, b, (((0,), (0,)), ((), ())), preferred_element_type=jnp.float32)


def halves(logits):
    small = jnp.exp(-jnp.abs(logits))
    loss = jnp.maximum(logits, 0.0) + jnp.log1p(small)
    chance = jnp.where(logits >= 0, 1.0, small) / (1.0 + small)
    return loss, chance


def kernel(
    groups, blocks,
    image, text, caption, log_scale, bias,
    grad_image, grad_text, row_loss,
    own_image, own_text, near_text, near_image, far_text, far_image, sum_image, sum_text,
    load_sem, send_sem, recv_sem,
):
    rows = image.shape[0]
    part = rows // CHUNKS
    me = lax.axis_index("dp") * groups + lax.axis_index("group")

    def device(step):
        at = lax.rem(me + step + blocks, blocks)
        return (at // groups, lax.rem(at, groups))

    far = blocks // 2 + 1
    flows = (
        (far_text, text, device(far)),
        (far_image, image, device(-far)),
        (near_text, text, device(groups)),
        (near_image, image, device(-groups)),
    )
    barrier = pltpu.get_barrier_semaphore()
    for _, _, peer in flows:
        pl.semaphore_signal(barrier, inc=1, device_id=peer, device_id_type=MESH)
    pl.semaphore_wait(barrier, len(flows))

    def copy(flow, k):
        target, source, peer = flows[flow]
        piece = pl.ds(pl.multiple_of(k * part, part), part)
        return pltpu.make_async_remote_copy(
            src_ref=source.at[piece],
            dst_ref=target.at[piece],
            send_sem=send_sem.at[flow, k],
            recv_sem=recv_sem.at[flow, k],
            device_id=peer,
            device_id_type=MESH,
        )

    for k in range(CHUNKS):
        for flow in range(len(flows)):
            copy(flow, k).start()

    loads = [
        pltpu.make_async_copy(image, own_image, load_sem.at[0]),
        pltpu.make_async_copy(text, own_text, load_sem.at[1]),
    ]
    for load in loads:
        load.start()
    for load in loads:
        load.wait()

    scale = jnp.exp(jnp.full((1, rows), log_scale[0], jnp.float32))
    shift = bias[0]

    row_loss[...] = jnp.zeros_like(row_loss)

    def own(k, _):
        piece = pl.ds(pl.multiple_of(k * part, part), part)
        texts = own_text[piece, :]
        logits = scale * dot_nt(texts, own_image[...]) + shift
        loss, chance = halves(logits)
        line = lax.broadcasted_iota(jnp.int32, (part, rows), 0) + k * part
        positive = line == caption[...]
        loss = loss - jnp.where(positive, logits, 0.0)
        coef = (chance - positive.astype(jnp.float32)).astype(jnp.bfloat16)
        row_loss[...] += jnp.sum(loss, axis=0, keepdims=True)
        sum_text[piece, :] = jnp.dot(coef, own_image[...], preferred_element_type=jnp.float32)
        add = dot_tn(coef, texts)

        @pl.when(k == 0)
        def _():
            sum_image[...] = add

        @pl.when(k > 0)
        def _():
            sum_image[...] += add

        return 0

    lax.fori_loop(0, CHUNKS, own, 0)

    def pair(flow_text, flow_image):
        def step(k, _):
            piece = pl.ds(pl.multiple_of(k * part, part), part)
            copy(flow_text, k).wait_recv()
            texts = flows[flow_text][0][piece, :]
            loss, chance = halves(scale * dot_nt(texts, own_image[...]) + shift)
            row_loss[...] += jnp.sum(loss, axis=0, keepdims=True)
            sum_image[...] += dot_tn(chance.astype(jnp.bfloat16), texts)
            copy(flow_image, k).wait_recv()
            images = flows[flow_image][0][piece, :]
            _, chance = halves(scale * dot_nt(images, own_text[...]) + shift)
            sum_text[...] += dot_tn(chance.astype(jnp.bfloat16), images)
            return 0

        lax.fori_loop(0, CHUNKS, step, 0)

    pair(2, 3)
    pair(0, 1)
    wide = jnp.exp(jnp.full((1, image.shape[1]), log_scale[0], jnp.float32))
    grad_image[...] = (wide * sum_image[...]).astype(grad_image.dtype)
    grad_text[...] = (wide * sum_text[...]).astype(grad_text.dtype)
    row_loss[...] = row_loss[...] / jnp.float32(3 * rows)

    def drain(k, _):
        for flow in range(len(flows)):
            copy(flow, k).wait_send()
        return 0

    lax.fori_loop(0, CHUNKS, drain, 0)


def solution(mesh):
    groups = mesh.shape["group"]
    blocks = mesh.shape["dp"] * groups

    def body(image, text, caption, log_scale, bias):
        rows, width = image.shape
        block = pltpu.VMEM((rows, width), jnp.bfloat16)
        total = pltpu.VMEM((rows, width), jnp.float32)
        vmem = pl.BlockSpec(memory_space=pltpu.VMEM)
        smem = pl.BlockSpec(memory_space=pltpu.SMEM)
        anywhere = pl.BlockSpec(memory_space=pl.ANY)
        grad_image, grad_text, row_loss = pl.pallas_call(
            functools.partial(kernel, groups, blocks),
            out_shape=(
                jax.ShapeDtypeStruct((rows, width), jnp.bfloat16),
                jax.ShapeDtypeStruct((rows, width), jnp.bfloat16),
                jax.ShapeDtypeStruct((1, rows), jnp.float32),
            ),
            in_specs=[anywhere, anywhere, vmem, smem, smem],
            out_specs=(vmem, vmem, vmem),
            scratch_shapes=[block] * 6
            + [total] * 2
            + [
                pltpu.SemaphoreType.DMA((2,)),
                pltpu.SemaphoreType.DMA((4, CHUNKS)),
                pltpu.SemaphoreType.DMA((4, CHUNKS)),
            ],
            compiler_params=pltpu.CompilerParams(
                collective_id=0, has_side_effects=True, vmem_limit_bytes=40 << 20
            ),
        )(image, text, caption, log_scale.reshape(1), bias.reshape(1))
        return grad_image, grad_text, row_loss.reshape(rows)

    spec = P(("dp", "group"), None)
    return jax.shard_map(
        body,
        mesh=mesh,
        in_specs=(spec, spec, spec, P(), P()),
        out_specs=(spec, spec, P(("dp", "group"))),
        check_vma=False,
    )
```

```python
import functools

import jax
import jax.numpy as jnp
from jax import lax
from jax.experimental import pallas as pl
from jax.experimental.pallas import tpu as pltpu
from jax.sharding import PartitionSpec as P

MESH = pl.DeviceIdType.MESH
CHUNKS = 4
XS, YS, ZS = 4, 8, 12
PLANE = XS * YS * 2
HOPS = ZS // 2


def dot_nt(a, b):
    return lax.dot_general(a, b, (((1,), (1,)), ((), ())), preferred_element_type=jnp.float32)


def dot_tn(a, b):
    return lax.dot_general(a, b, (((0,), (0,)), ((), ())), preferred_element_type=jnp.float32)


def halves(logits):
    small = jnp.exp(-jnp.abs(logits))
    loss = jnp.maximum(logits, 0.0) + jnp.log1p(small)
    chance = jnp.where(logits >= 0, 1.0, small) / (1.0 + small)
    return loss, chance


def kernel(
    groups, blocks,
    image, text, caption, log_scale, bias,
    grad_image, grad_text, row_loss,
    own_image, own_text, near_text, near_image, far_text, far_image,
    near_pass, far_pass, sum_image, sum_text,
    load_sem, far_send, far_recv, near_send, near_recv, pass_send, pass_recv,
):
    rows = image.shape[0]
    part = rows // CHUNKS
    me = lax.axis_index("dp") * groups + lax.axis_index("group")
    z, x, y, core = me // PLANE, lax.rem(me // (2 * YS), XS), lax.rem(me // 2, YS), lax.rem(me, 2)

    def block(at):
        at = lax.rem(at + blocks, blocks)
        return (at // groups, lax.rem(at, groups))

    def place(z, x, y, core):
        return block(((z * XS + x) * YS + y) * 2 + core)

    high = y // (YS // 2)
    edge = (XS - 1) * high
    across = 2 * high - 1
    opposite = y - across * (YS // 2)
    is_edge = x == edge
    plane_at = lax.rem(me, PLANE)
    last = plane_at == PLANE - 1
    first = plane_at == 0
    text_pass = jnp.logical_and(y == 0, core == 0)
    image_pass = jnp.logical_and(y == YS - 1, core == 1)

    near_source = place(z, edge, y, core)
    near_goal = place(z + across, XS - 1 - edge, opposite, core)

    def near_stop(q):
        return place(z, q, y, core)

    def near_sender(q):
        return place(z + across, q, opposite, core)

    text_source = place(z, XS - 1, YS - 1, 1)
    text_goal = place(z + 2, 0, 0, 0)
    image_source = place(z, 0, 0, 0)
    image_goal = place(z - 2, XS - 1, YS - 1, 1)

    def text_stop(j):
        return place(z, j, 0, 0)

    def image_stop(j):
        return place(z, j, YS - 1, 1)

    leap = PLANE + 1
    regular = [block(me + step) for step in (leap, -leap, PLANE, -PLANE, groups, -groups)]
    barrier = pltpu.get_barrier_semaphore()

    def greet(peers):
        for peer in peers:
            pl.semaphore_signal(barrier, inc=1, device_id=peer, device_id_type=MESH)

    greet(regular)

    @pl.when(is_edge)
    def _():
        for n in range(1, XS):
            greet([near_stop(edge - across * n), near_sender(XS - 1 - edge + across * n)])

    @pl.when(jnp.logical_not(is_edge))
    def _():
        greet([near_source, near_goal])

    @pl.when(last)
    def _():
        greet([text_stop(j) for j in range(XS)] + [place(z + 2, j, YS - 1, 1) for j in range(XS)])

    @pl.when(first)
    def _():
        greet([image_stop(j) for j in range(XS)] + [place(z - 2, j, 0, 0) for j in range(XS)])

    @pl.when(text_pass)
    def _():
        greet([text_source, text_goal])

    @pl.when(image_pass)
    def _():
        greet([image_source, image_goal])

    def one_if(condition):
        return condition.astype(jnp.int32)

    pl.semaphore_wait(
        barrier,
        len(regular) + 2
        + (2 * XS - 4) * one_if(is_edge)
        + 2 * XS * (one_if(last) + one_if(first))
        + 2 * (one_if(text_pass) + one_if(image_pass)),
    )

    def rows_of(k):
        return pl.ds(pl.multiple_of(k * part, part), part)

    def send(source, target, sent, got, peer):
        return pltpu.make_async_remote_copy(
            src_ref=source, dst_ref=target, send_sem=sent, recv_sem=got,
            device_id=peer, device_id_type=MESH,
        )

    inputs = (text, image)
    far_bufs = (far_text, far_image)
    near_bufs = (near_text, near_image)

    def far_first(flow, k, peer=None, source=None, sent=None):
        return send(
            inputs[flow].at[rows_of(k)] if source is None else source,
            far_bufs[flow].at[0, rows_of(k)],
            far_send.at[flow, 0, k] if sent is None else sent,
            far_recv.at[flow, 0, k],
            block(me + (leap, -leap)[flow]) if peer is None else peer,
        )

    def far_next(flow, s, k):
        return send(
            far_bufs[flow].at[s - 1, rows_of(k)], far_bufs[flow].at[s, rows_of(k)],
            far_send.at[flow, s, k], far_recv.at[flow, s, k], block(me + (PLANE, -PLANE)[flow]),
        )

    def near(flow, k, peer=None, source=None, sent=None):
        return send(
            inputs[flow].at[rows_of(k)] if source is None else source,
            near_bufs[flow].at[rows_of(k)],
            near_send.at[flow, k] if sent is None else sent,
            near_recv.at[flow, k],
            block(me + (groups, -groups)[flow]) if peer is None else peer,
        )

    def near_detour(flow, k):
        return send(
            inputs[flow].at[rows_of(k)], near_pass, near_send.at[flow, k], pass_recv.at[0], near_stop(k)
        )

    def far_detour(flow, k):
        return send(
            inputs[flow].at[rows_of(k)], far_pass, far_send.at[flow, 0, k], pass_recv.at[1],
            (text_stop, image_stop)[flow](k),
        )

    far_special = (last, first)
    near_special = (
        jnp.logical_and(is_edge, high == 1),
        jnp.logical_and(is_edge, high == 0),
    )

    for flow in (0, 1):
        @pl.when(far_special[flow])
        def _():
            if flow == 0:
                for k in range(CHUNKS):
                    far_detour(flow, k).start()
            else:
                for k in reversed(range(CHUNKS)):
                    far_detour(flow, k).start()

        @pl.when(near_special[flow])
        def _():
            for k in range(CHUNKS):
                if k == (XS - 1, 0)[flow]:
                    near(flow, k).start()
                else:
                    near_detour(flow, k).start()

    def open_far(k, _):
        for flow in (0, 1):
            @pl.when(jnp.logical_not(far_special[flow]))
            def _():
                far_first(flow, k).start()

        return 0

    def open_near(k, _):
        for flow in (0, 1):
            @pl.when(jnp.logical_not(near_special[flow]))
            def _():
                near(flow, k).start()

        return 0

    lax.fori_loop(0, CHUNKS, open_far, 0)
    lax.fori_loop(0, CHUNKS, open_near, 0)

    loads = [
        pltpu.make_async_copy(image, own_image, load_sem.at[0]),
        pltpu.make_async_copy(text, own_text, load_sem.at[1]),
    ]
    for load in loads:
        load.start()

    text_hand = far_first(0, x, text_goal, far_pass, pass_send.at[1])
    image_hand = far_first(1, x, image_goal, far_pass, pass_send.at[1])
    near_text_hand = near(0, x, near_goal, near_pass, pass_send.at[0])
    near_image_hand = near(1, x, near_goal, near_pass, pass_send.at[0])
    pass_text = jnp.logical_and(jnp.logical_not(is_edge), high == 1)
    pass_image = jnp.logical_and(jnp.logical_not(is_edge), high == 0)
    hands = (
        (text_pass, text_hand),
        (image_pass, image_hand),
        (pass_text, near_text_hand),
        (pass_image, near_image_hand),
    )

    for n, (mine, hand) in enumerate(hands):
        @pl.when(mine)
        def _():
            send(
                text.at[rows_of(0)], (far_pass, near_pass)[n // 2], pass_send.at[1 - n // 2],
                pass_recv.at[1 - n // 2], block(me + groups),
            ).wait_recv()
            hand.start()

    def forward(i, _):
        s, k = i // CHUNKS, lax.rem(i, CHUNKS)
        for flow in (0, 1):
            @pl.when(s == 1)
            def _():
                far_first(flow, k).wait_recv()

            @pl.when(s > 1)
            def _():
                far_next(flow, s - 1, k).wait_recv()

            far_next(flow, s, k).start()
        return 0

    lax.fori_loop(CHUNKS, 2 * CHUNKS, forward, 0)
    for load in loads:
        load.wait()

    scale = jnp.exp(jnp.full((1, rows), log_scale[0], jnp.float32))
    shift = bias[0]
    row_loss[...] = jnp.zeros_like(row_loss)

    def own(k, _):
        texts = own_text[rows_of(k), :]
        logits = scale * dot_nt(texts, own_image[...]) + shift
        loss, chance = halves(logits)
        line = lax.broadcasted_iota(jnp.int32, (part, rows), 0) + k * part
        positive = line == caption[...]
        loss = loss - jnp.where(positive, logits, 0.0)
        coef = (chance - positive.astype(jnp.float32)).astype(jnp.bfloat16)
        row_loss[...] += jnp.sum(loss, axis=0, keepdims=True)
        sum_text[rows_of(k), :] = jnp.dot(coef, own_image[...], preferred_element_type=jnp.float32)
        add = dot_tn(coef, texts)

        @pl.when(k == 0)
        def _():
            sum_image[...] = add

        @pl.when(k > 0)
        def _():
            sum_image[...] += add

        return 0

    lax.fori_loop(0, CHUNKS, own, 0)
    lax.fori_loop(2 * CHUNKS, HOPS * CHUNKS, forward, 0)

    def meet_text(texts):
        loss, chance = halves(scale * dot_nt(texts, own_image[...]) + shift)
        row_loss[...] += jnp.sum(loss, axis=0, keepdims=True)
        sum_image[...] += dot_tn(chance.astype(jnp.bfloat16), texts)

    def meet_image(images):
        _, chance = halves(scale * dot_nt(images, own_text[...]) + shift)
        sum_text[...] += dot_tn(chance.astype(jnp.bfloat16), images)

    def near_pair(k, _):
        near(0, k).wait_recv()
        meet_text(near_text[rows_of(k), :])
        near(1, k).wait_recv()
        meet_image(near_image[rows_of(k), :])
        return 0

    def far_pair(k, _):
        far_next(0, HOPS - 1, k).wait_recv()
        meet_text(far_text[HOPS - 1, rows_of(k), :])
        far_next(1, HOPS - 1, k).wait_recv()
        meet_image(far_image[HOPS - 1, rows_of(k), :])
        return 0

    lax.fori_loop(0, CHUNKS, near_pair, 0)
    lax.fori_loop(0, CHUNKS, far_pair, 0)
    wide = jnp.exp(jnp.full((1, image.shape[1]), log_scale[0], jnp.float32))
    grad_image[...] = (wide * sum_image[...]).astype(grad_image.dtype)
    grad_text[...] = (wide * sum_text[...]).astype(grad_text.dtype)
    row_loss[...] = row_loss[...] / jnp.float32(3 * rows)

    def drain(k, _):
        for flow in (0, 1):
            far_first(flow, k).wait_send()
            near(flow, k).wait_send()
        return 0

    def drain_next(i, _):
        for flow in (0, 1):
            far_next(flow, i // CHUNKS, lax.rem(i, CHUNKS)).wait_send()
        return 0

    lax.fori_loop(0, CHUNKS, drain, 0)
    lax.fori_loop(CHUNKS, HOPS * CHUNKS, drain_next, 0)
    for mine, hand in hands:
        @pl.when(mine)
        def _():
            hand.wait_send()


def solution(mesh):
    groups = mesh.shape["group"]
    blocks = mesh.shape["dp"] * groups

    def body(image, text, caption, log_scale, bias):
        rows, width = image.shape
        block = pltpu.VMEM((rows, width), jnp.bfloat16)
        relayed = pltpu.VMEM((HOPS, rows, width), jnp.bfloat16)
        piece = pltpu.VMEM((rows // CHUNKS, width), jnp.bfloat16)
        total = pltpu.VMEM((rows, width), jnp.float32)
        vmem = pl.BlockSpec(memory_space=pltpu.VMEM)
        smem = pl.BlockSpec(memory_space=pltpu.SMEM)
        anywhere = pl.BlockSpec(memory_space=pl.ANY)
        grad_image, grad_text, row_loss = pl.pallas_call(
            functools.partial(kernel, groups, blocks),
            out_shape=(
                jax.ShapeDtypeStruct((rows, width), jnp.bfloat16),
                jax.ShapeDtypeStruct((rows, width), jnp.bfloat16),
                jax.ShapeDtypeStruct((1, rows), jnp.float32),
            ),
            in_specs=[anywhere, anywhere, vmem, smem, smem],
            out_specs=(vmem, vmem, vmem),
            scratch_shapes=[block] * 4
            + [relayed] * 2
            + [piece] * 2
            + [total] * 2
            + [
                pltpu.SemaphoreType.DMA((2,)),
                pltpu.SemaphoreType.DMA((2, HOPS, CHUNKS)),
                pltpu.SemaphoreType.DMA((2, HOPS, CHUNKS)),
                pltpu.SemaphoreType.DMA((2, CHUNKS)),
                pltpu.SemaphoreType.DMA((2, CHUNKS)),
                pltpu.SemaphoreType.DMA((2,)),
                pltpu.SemaphoreType.DMA((2,)),
            ],
            compiler_params=pltpu.CompilerParams(
                collective_id=0, has_side_effects=True, vmem_limit_bytes=58 << 20
            ),
        )(image, text, caption, log_scale.reshape(1), bias.reshape(1))
        return grad_image, grad_text, row_loss.reshape(rows)

    spec = P(("dp", "group"), None)
    return jax.shard_map(
        body,
        mesh=mesh,
        in_specs=(spec, spec, spec, P(), P()),
        out_specs=(spec, spec, P(("dp", "group"))),
        check_vma=False,
    )
```

```python
import functools

import jax
import jax.numpy as jnp
from jax import lax
from jax.experimental import pallas as pl
from jax.experimental.pallas import tpu as pltpu
from jax.sharding import PartitionSpec as P

MESH = pl.DeviceIdType.MESH
CHUNKS = 4
XS, YS, ZS = 4, 8, 12
PLANE = XS * YS * 2
HOPS = ZS // 2


def dot_nt(a, b):
    return lax.dot_general(a, b, (((1,), (1,)), ((), ())), preferred_element_type=jnp.float32)


def dot_tn(a, b):
    return lax.dot_general(a, b, (((0,), (0,)), ((), ())), preferred_element_type=jnp.float32)


def halves(logits):
    small = jnp.exp(-jnp.abs(logits))
    loss = jnp.maximum(logits, 0.0) + jnp.log1p(small)
    chance = jnp.where(logits >= 0, 1.0, small) / (1.0 + small)
    return loss, chance


def kernel(
    groups, blocks,
    image, text, caption, log_scale, bias,
    grad_image, grad_text, row_loss,
    own_image, own_text, near_text, near_image, far_text, far_image,
    near_pass, far_pass, sum_image, sum_text,
    load_sem, far_send, far_recv, near_send, near_recv, pass_send, pass_recv,
):
    rows = image.shape[0]
    part = rows // CHUNKS
    me = lax.axis_index("dp") * groups + lax.axis_index("group")
    z, x, y, core = me // PLANE, lax.rem(me // (2 * YS), XS), lax.rem(me // 2, YS), lax.rem(me, 2)

    def block(at):
        at = lax.rem(at + blocks, blocks)
        return (at // groups, lax.rem(at, groups))

    def place(z, x, y, core):
        return block(((z * XS + x) * YS + y) * 2 + core)

    high = y // (YS // 2)
    edge = (XS - 1) * high
    across = 2 * high - 1
    opposite = y - across * (YS // 2)
    is_edge = x == edge
    plane_at = lax.rem(me, PLANE)
    last = plane_at == PLANE - 1
    first = plane_at == 0
    text_pass = jnp.logical_and(y == 0, core == 0)
    image_pass = jnp.logical_and(y == YS - 1, core == 1)

    near_source = place(z, edge, y, core)
    near_goal = place(z + across, XS - 1 - edge, opposite, core)

    def near_stop(q):
        return place(z, q, y, core)

    def near_sender(q):
        return place(z + across, q, opposite, core)

    text_source = place(z, XS - 1, YS - 1, 1)
    text_goal = place(z + 2, 0, 0, 0)
    image_source = place(z, 0, 0, 0)
    image_goal = place(z - 2, XS - 1, YS - 1, 1)

    def text_stop(j):
        return place(z, j, 0, 0)

    def image_stop(j):
        return place(z, j, YS - 1, 1)

    leap = PLANE + 1
    barrier = pltpu.get_barrier_semaphore()

    def one_if(condition):
        return condition.astype(jnp.int32)

    def tell(peers):
        for peer in peers:
            pl.semaphore_signal(barrier, inc=1, device_id=peer, device_id_type=MESH)

    top = z == ZS - 1
    goal_edge = jnp.logical_and(is_edge, high == 1)
    senders = [(step, block(me - step)) for step in (PLANE, groups)]
    others = [(step, block(me + step)) for step in (PLANE, groups)]

    for step, peer in senders:
        @pl.when(me >= step)
        def _():
            tell([peer])

    @pl.when(jnp.logical_and(jnp.logical_not(first), me >= leap))
    def _():
        tell([block(me - leap)])

    for step, peer in others:
        @pl.when(me + step < blocks)
        def _():
            tell([peer])

    @pl.when(jnp.logical_and(jnp.logical_not(last), me + leap < blocks))
    def _():
        tell([block(me + leap)])

    @pl.when(is_edge)
    def _():
        for n in range(1, XS):
            @pl.when(jnp.logical_not(jnp.logical_and(top, high == 1)))
            def _():
                tell([near_sender(XS - 1 - edge + across * n)])

    low_pass = jnp.logical_and(jnp.logical_not(is_edge), high == 0)

    @pl.when(jnp.logical_not(is_edge))
    def _():
        tell([near_source])

    image_senders = [place(z + 2, j, YS - 1, 1) for j in range(XS)]

    @pl.when(jnp.logical_and(last, z < ZS - 2))
    def _():
        tell(image_senders)

    @pl.when(first)
    def _():
        tell([place(z - 2, j, 0, 0) for j in range(XS)])

    @pl.when(text_pass)
    def _():
        tell([text_source])

    @pl.when(image_pass)
    def _():
        tell([image_source])

    late_count = (
        one_if(z == 0) * (1 + one_if(jnp.logical_not(first)))
        + one_if(me < groups)
        + one_if(jnp.logical_and(low_pass, z == 0))
        + one_if(jnp.logical_and(image_pass, z < 2))
    )
    pl.semaphore_wait(
        barrier,
        6 - one_if(first) - one_if(last)
        + (XS - 1) * one_if(is_edge) + one_if(jnp.logical_not(is_edge))
        + XS * (one_if(last) + one_if(first))
        + one_if(text_pass) + one_if(image_pass)
        + (XS - 1) * one_if(jnp.logical_and(goal_edge, top))
        + XS * one_if(jnp.logical_and(last, z >= ZS - 2))
        - late_count,
    )

    for step, peer in senders:
        @pl.when(me < step)
        def _():
            tell([peer])

    @pl.when(jnp.logical_and(jnp.logical_not(first), me < leap))
    def _():
        tell([block(me - leap)])

    @pl.when(jnp.logical_and(low_pass, z == 0))
    def _():
        tell([near_goal])

    @pl.when(jnp.logical_and(image_pass, z < 2))
    def _():
        tell([image_goal])

    for step, peer in others:
        @pl.when(me + step >= blocks)
        def _():
            tell([peer])

    @pl.when(jnp.logical_and(jnp.logical_not(last), me + leap >= blocks))
    def _():
        tell([block(me + leap)])

    @pl.when(jnp.logical_and(goal_edge, top))
    def _():
        tell([near_sender(n) for n in range(1, XS)])

    @pl.when(jnp.logical_and(last, z >= ZS - 2))
    def _():
        tell(image_senders)

    def rows_of(k):
        return pl.ds(pl.multiple_of(k * part, part), part)

    def send(source, target, sent, got, peer):
        return pltpu.make_async_remote_copy(
            src_ref=source, dst_ref=target, send_sem=sent, recv_sem=got,
            device_id=peer, device_id_type=MESH,
        )

    inputs = (text, image)
    far_bufs = (far_text, far_image)
    near_bufs = (near_text, near_image)

    def far_first(flow, k, peer=None, source=None, sent=None):
        return send(
            inputs[flow].at[rows_of(k)] if source is None else source,
            far_bufs[flow].at[0, rows_of(k)],
            far_send.at[flow, 0, k] if sent is None else sent,
            far_recv.at[flow, 0, k],
            block(me + (leap, -leap)[flow]) if peer is None else peer,
        )

    def far_next(flow, s, k):
        return send(
            far_bufs[flow].at[s - 1, rows_of(k)], far_bufs[flow].at[s, rows_of(k)],
            far_send.at[flow, s, k], far_recv.at[flow, s, k], block(me + (PLANE, -PLANE)[flow]),
        )

    def near(flow, k, peer=None, source=None, sent=None):
        return send(
            inputs[flow].at[rows_of(k)] if source is None else source,
            near_bufs[flow].at[rows_of(k)],
            near_send.at[flow, k] if sent is None else sent,
            near_recv.at[flow, k],
            block(me + (groups, -groups)[flow]) if peer is None else peer,
        )

    def near_detour(flow, k):
        return send(
            inputs[flow].at[rows_of(k)], near_pass, near_send.at[flow, k], pass_recv.at[0], near_stop(k)
        )

    def far_detour(flow, k):
        return send(
            inputs[flow].at[rows_of(k)], far_pass, far_send.at[flow, 0, k], pass_recv.at[1],
            (text_stop, image_stop)[flow](k),
        )

    far_special = (last, first)
    near_special = (
        jnp.logical_and(is_edge, high == 1),
        jnp.logical_and(is_edge, high == 0),
    )

    def open_special(flow):
        @pl.when(far_special[flow])
        def _():
            for k in range(CHUNKS):
                far_detour(flow, k if flow == 0 else CHUNKS - 1 - k).start()

        @pl.when(near_special[flow])
        def _():
            for k in range(CHUNKS):
                if k == (XS - 1, 0)[flow]:
                    near(flow, k).start()
                else:
                    near_detour(flow, k).start()

    def open_flows(flows):
        def open_far(k, _):
            for flow in flows:
                @pl.when(jnp.logical_not(far_special[flow]))
                def _():
                    far_first(flow, k).start()

            return 0

        def open_near(k, _):
            for flow in flows:
                @pl.when(jnp.logical_not(near_special[flow]))
                def _():
                    near(flow, k).start()

            return 0

        for flow in flows:
            open_special(flow)
        lax.fori_loop(0, CHUNKS, open_far, 0)
        lax.fori_loop(0, CHUNKS, open_near, 0)

    @pl.when(z > 0)
    def _():
        open_flows((0, 1))

    @pl.when(z == 0)
    def _():
        open_flows((0,))

    @pl.when(late_count > 0)
    def _():
        pl.semaphore_wait(barrier, late_count)

    @pl.when(z == 0)
    def _():
        open_flows((1,))

    loads = [
        pltpu.make_async_copy(image, own_image, load_sem.at[0]),
        pltpu.make_async_copy(text, own_text, load_sem.at[1]),
    ]
    for load in loads:
        load.start()

    text_hand = far_first(0, x, text_goal, far_pass, pass_send.at[1])
    image_hand = far_first(1, x, image_goal, far_pass, pass_send.at[1])
    near_text_hand = near(0, x, near_goal, near_pass, pass_send.at[0])
    near_image_hand = near(1, x, near_goal, near_pass, pass_send.at[0])
    pass_text = jnp.logical_and(jnp.logical_not(is_edge), high == 1)
    pass_image = jnp.logical_and(jnp.logical_not(is_edge), high == 0)
    hands = (
        (text_pass, text_hand),
        (image_pass, image_hand),
        (pass_text, near_text_hand),
        (pass_image, near_image_hand),
    )

    for n, (mine, hand) in enumerate(hands):
        @pl.when(mine)
        def _():
            send(
                text.at[rows_of(0)], (far_pass, near_pass)[n // 2], pass_send.at[1 - n // 2],
                pass_recv.at[1 - n // 2], block(me + groups),
            ).wait_recv()
            hand.start()

    def forward(i, _):
        s, k = i // CHUNKS, lax.rem(i, CHUNKS)
        for flow in (0, 1):
            @pl.when(s == 1)
            def _():
                far_first(flow, k).wait_recv()

            @pl.when(s > 1)
            def _():
                far_next(flow, s - 1, k).wait_recv()

            far_next(flow, s, k).start()
        return 0

    lax.fori_loop(CHUNKS, 2 * CHUNKS, forward, 0)
    for load in loads:
        load.wait()

    scale = jnp.exp(jnp.full((1, rows), log_scale[0], jnp.float32))
    shift = bias[0]
    row_loss[...] = jnp.zeros_like(row_loss)

    def own(k, _):
        texts = own_text[rows_of(k), :]
        logits = scale * dot_nt(texts, own_image[...]) + shift
        loss, chance = halves(logits)
        line = lax.broadcasted_iota(jnp.int32, (part, rows), 0) + k * part
        positive = line == caption[...]
        loss = loss - jnp.where(positive, logits, 0.0)
        coef = (chance - positive.astype(jnp.float32)).astype(jnp.bfloat16)
        row_loss[...] += jnp.sum(loss, axis=0, keepdims=True)
        sum_text[rows_of(k), :] = jnp.dot(coef, own_image[...], preferred_element_type=jnp.float32)
        add = dot_tn(coef, texts)

        @pl.when(k == 0)
        def _():
            sum_image[...] = add

        @pl.when(k > 0)
        def _():
            sum_image[...] += add

        return 0

    lax.fori_loop(0, CHUNKS, own, 0)
    lax.fori_loop(2 * CHUNKS, HOPS * CHUNKS, forward, 0)

    def meet_text(texts):
        loss, chance = halves(scale * dot_nt(texts, own_image[...]) + shift)
        row_loss[...] += jnp.sum(loss, axis=0, keepdims=True)
        sum_image[...] += dot_tn(chance.astype(jnp.bfloat16), texts)

    def meet_image(images):
        _, chance = halves(scale * dot_nt(images, own_text[...]) + shift)
        sum_text[...] += dot_tn(chance.astype(jnp.bfloat16), images)

    def near_pair(k, _):
        near(0, k).wait_recv()
        meet_text(near_text[rows_of(k), :])
        near(1, k).wait_recv()
        meet_image(near_image[rows_of(k), :])
        return 0

    def far_pair(k, _):
        far_next(0, HOPS - 1, k).wait_recv()
        meet_text(far_text[HOPS - 1, rows_of(k), :])
        far_next(1, HOPS - 1, k).wait_recv()
        meet_image(far_image[HOPS - 1, rows_of(k), :])
        return 0

    lax.fori_loop(0, CHUNKS, near_pair, 0)
    lax.fori_loop(0, CHUNKS, far_pair, 0)
    wide = jnp.exp(jnp.full((1, image.shape[1]), log_scale[0], jnp.float32))
    grad_image[...] = (wide * sum_image[...]).astype(grad_image.dtype)
    grad_text[...] = (wide * sum_text[...]).astype(grad_text.dtype)
    row_loss[...] = row_loss[...] / jnp.float32(3 * rows)

    def drain(k, _):
        for flow in (0, 1):
            far_first(flow, k).wait_send()
            near(flow, k).wait_send()
        return 0

    def drain_next(i, _):
        for flow in (0, 1):
            far_next(flow, i // CHUNKS, lax.rem(i, CHUNKS)).wait_send()
        return 0

    lax.fori_loop(0, CHUNKS, drain, 0)
    lax.fori_loop(CHUNKS, HOPS * CHUNKS, drain_next, 0)
    for mine, hand in hands:
        @pl.when(mine)
        def _():
            hand.wait_send()


def solution(mesh):
    groups = mesh.shape["group"]
    blocks = mesh.shape["dp"] * groups

    def body(image, text, caption, log_scale, bias):
        rows, width = image.shape
        block = pltpu.VMEM((rows, width), jnp.bfloat16)
        relayed = pltpu.VMEM((HOPS, rows, width), jnp.bfloat16)
        piece = pltpu.VMEM((rows // CHUNKS, width), jnp.bfloat16)
        total = pltpu.VMEM((rows, width), jnp.float32)
        vmem = pl.BlockSpec(memory_space=pltpu.VMEM)
        smem = pl.BlockSpec(memory_space=pltpu.SMEM)
        anywhere = pl.BlockSpec(memory_space=pl.ANY)
        grad_image, grad_text, row_loss = pl.pallas_call(
            functools.partial(kernel, groups, blocks),
            out_shape=(
                jax.ShapeDtypeStruct((rows, width), jnp.bfloat16),
                jax.ShapeDtypeStruct((rows, width), jnp.bfloat16),
                jax.ShapeDtypeStruct((1, rows), jnp.float32),
            ),
            in_specs=[anywhere, anywhere, vmem, smem, smem],
            out_specs=(vmem, vmem, vmem),
            scratch_shapes=[block] * 4
            + [relayed] * 2
            + [piece] * 2
            + [total] * 2
            + [
                pltpu.SemaphoreType.DMA((2,)),
                pltpu.SemaphoreType.DMA((2, HOPS, CHUNKS)),
                pltpu.SemaphoreType.DMA((2, HOPS, CHUNKS)),
                pltpu.SemaphoreType.DMA((2, CHUNKS)),
                pltpu.SemaphoreType.DMA((2, CHUNKS)),
                pltpu.SemaphoreType.DMA((2,)),
                pltpu.SemaphoreType.DMA((2,)),
            ],
            compiler_params=pltpu.CompilerParams(
                collective_id=0, has_side_effects=True, vmem_limit_bytes=54_250_000
            ),
        )(image, text, caption, log_scale.reshape(1), bias.reshape(1))
        return grad_image, grad_text, row_loss.reshape(rows)

    spec = P(("dp", "group"), None)
    return jax.shard_map(
        body,
        mesh=mesh,
        in_specs=(spec, spec, spec, P(), P()),
        out_specs=(spec, spec, P(("dp", "group"))),
        check_vma=False,
    )
```

```python
import functools

import jax
import jax.numpy as jnp
from jax import lax
from jax.experimental import pallas as pl
from jax.experimental.pallas import tpu as pltpu
from jax.sharding import PartitionSpec as P

MESH = pl.DeviceIdType.MESH
CHUNKS = 4
XS, YS, ZS = 4, 8, 12
PLANE = XS * YS * 2
HOPS = ZS // 2
TURNED = 1


def dot_nt(a, b):
    return lax.dot_general(a, b, (((1,), (1,)), ((), ())), preferred_element_type=jnp.float32)


def dot_tn(a, b):
    return lax.dot_general(a, b, (((0,), (0,)), ((), ())), preferred_element_type=jnp.float32)


def halves(logits):
    small = jnp.exp(-jnp.abs(logits))
    loss = jnp.maximum(logits, 0.0) + jnp.log1p(small)
    chance = jnp.where(logits >= 0, 1.0, small) / (1.0 + small)
    return loss, chance


def kernel(
    groups, blocks,
    image, text, caption, log_scale, bias,
    grad_image, grad_text, loss_out,
    own_image, own_text, near_text, near_image, far_text, far_image,
    near_pass, far_pass, turned, sum_image, sum_text, row_loss,
    load_sem, far_send, far_recv, near_send, near_recv, pass_send, pass_recv, turned_sem,
):
    rows = image.shape[0]
    part = rows // CHUNKS
    me = lax.axis_index("dp") * groups + lax.axis_index("group")
    z, x, y, core = me // PLANE, lax.rem(me // (2 * YS), XS), lax.rem(me // 2, YS), lax.rem(me, 2)

    def block(at):
        at = lax.rem(at + blocks, blocks)
        return (at // groups, lax.rem(at, groups))

    def place(z, x, y, core):
        return block(((z * XS + x) * YS + y) * 2 + core)

    high = y // (YS // 2)
    edge = (XS - 1) * high
    across = 2 * high - 1
    opposite = y - across * (YS // 2)
    is_edge = x == edge
    plane_at = lax.rem(me, PLANE)
    last = plane_at == PLANE - 1
    first = plane_at == 0
    text_pass = jnp.logical_and(y == 0, core == 0)
    image_pass = jnp.logical_and(y == YS - 1, core == 1)

    near_source = place(z, edge, y, core)
    near_goal = place(z + across, XS - 1 - edge, opposite, core)

    def near_stop(q):
        return place(z, q, y, core)

    def near_sender(q):
        return place(z + across, q, opposite, core)

    text_source = place(z, XS - 1, YS - 1, 1)
    text_goal = place(z + 2, 0, 0, 0)
    image_source = place(z, 0, 0, 0)
    image_goal = place(z - 2, XS - 1, YS - 1, 1)

    def text_stop(j):
        return place(z, j, 0, 0)

    def image_stop(j):
        return place(z, j, YS - 1, 1)

    leap = PLANE + 1
    barrier = pltpu.get_barrier_semaphore()

    def one_if(condition):
        return condition.astype(jnp.int32)

    def tell(peers):
        for peer in peers:
            pl.semaphore_signal(barrier, inc=1, device_id=peer, device_id_type=MESH)

    top = z == ZS - 1
    goal_edge = jnp.logical_and(is_edge, high == 1)
    senders = [(step, block(me - step)) for step in (PLANE, groups)]
    others = [(step, block(me + step)) for step in (PLANE, groups)]

    for step, peer in senders:
        @pl.when(me >= step)
        def _():
            tell([peer])

    @pl.when(jnp.logical_and(jnp.logical_not(first), me >= leap))
    def _():
        tell([block(me - leap)])

    for step, peer in others:
        @pl.when(me + step < blocks)
        def _():
            tell([peer])

    @pl.when(jnp.logical_and(jnp.logical_not(last), me + leap < blocks))
    def _():
        tell([block(me + leap)])

    @pl.when(is_edge)
    def _():
        for n in range(1, XS):
            @pl.when(jnp.logical_not(jnp.logical_and(top, high == 1)))
            def _():
                tell([near_sender(XS - 1 - edge + across * n)])

    low_pass = jnp.logical_and(jnp.logical_not(is_edge), high == 0)

    @pl.when(jnp.logical_not(is_edge))
    def _():
        tell([near_source])

    image_senders = [place(z + 2, j, YS - 1, 1) for j in range(XS)]

    @pl.when(jnp.logical_and(last, z < ZS - 2))
    def _():
        tell(image_senders)

    @pl.when(first)
    def _():
        tell([place(z - 2, j, 0, 0) for j in range(XS)])

    @pl.when(text_pass)
    def _():
        tell([text_source])

    @pl.when(image_pass)
    def _():
        tell([image_source])

    low_mid = z == HOPS - 1
    high_mid = z == HOPS
    text_turn = jnp.logical_and(high_mid, jnp.logical_not(last))
    image_turn = jnp.logical_and(low_mid, jnp.logical_not(first))
    text_turn_pass = jnp.logical_and(jnp.logical_and(text_pass, low_mid), x == TURNED)
    image_turn_pass = jnp.logical_and(jnp.logical_and(image_pass, high_mid), x == TURNED)
    text_turn_to = block(me - PLANE + 1)
    image_turn_to = block(me + PLANE - 1)

    @pl.when(text_turn)
    def _():
        tell([text_turn_to])

    @pl.when(image_turn)
    def _():
        tell([image_turn_to])

    @pl.when(jnp.logical_and(first, low_mid))
    def _():
        tell([text_stop(TURNED)])

    @pl.when(jnp.logical_and(last, high_mid))
    def _():
        tell([image_stop(TURNED)])

    late_count = (
        one_if(z == 0) * (1 + one_if(jnp.logical_not(first)))
        + one_if(me < groups)
        + one_if(jnp.logical_and(low_pass, z == 0))
        + one_if(jnp.logical_and(image_pass, z < 2))
    )
    pl.semaphore_wait(
        barrier,
        6 - one_if(first) - one_if(last)
        + (XS - 1) * one_if(is_edge) + one_if(jnp.logical_not(is_edge))
        + XS * (one_if(last) + one_if(first))
        + one_if(text_pass) + one_if(image_pass)
        + (XS - 1) * one_if(jnp.logical_and(goal_edge, top))
        + XS * one_if(jnp.logical_and(last, z >= ZS - 2))
        + one_if(text_turn) + one_if(image_turn)
        + one_if(text_turn_pass) + one_if(image_turn_pass)
        - late_count,
    )

    for step, peer in senders:
        @pl.when(me < step)
        def _():
            tell([peer])

    @pl.when(jnp.logical_and(jnp.logical_not(first), me < leap))
    def _():
        tell([block(me - leap)])

    @pl.when(jnp.logical_and(low_pass, z == 0))
    def _():
        tell([near_goal])

    @pl.when(jnp.logical_and(image_pass, z < 2))
    def _():
        tell([image_goal])

    for step, peer in others:
        @pl.when(me + step >= blocks)
        def _():
            tell([peer])

    @pl.when(jnp.logical_and(jnp.logical_not(last), me + leap >= blocks))
    def _():
        tell([block(me + leap)])

    @pl.when(jnp.logical_and(goal_edge, top))
    def _():
        tell([near_sender(n) for n in range(1, XS)])

    @pl.when(jnp.logical_and(last, z >= ZS - 2))
    def _():
        tell(image_senders)

    def rows_of(k):
        return pl.ds(pl.multiple_of(k * part, part), part)

    def send(source, target, sent, got, peer):
        return pltpu.make_async_remote_copy(
            src_ref=source, dst_ref=target, send_sem=sent, recv_sem=got,
            device_id=peer, device_id_type=MESH,
        )

    inputs = (text, image)
    far_bufs = (far_text, far_image)
    near_bufs = (near_text, near_image)

    def far_first(flow, k, peer=None, source=None, sent=None):
        return send(
            inputs[flow].at[rows_of(k)] if source is None else source,
            far_bufs[flow].at[0, rows_of(k)],
            far_send.at[flow, 0, k] if sent is None else sent,
            far_recv.at[flow, 0, k],
            block(me + (leap, -leap)[flow]) if peer is None else peer,
        )

    def far_next(flow, s, k):
        return send(
            far_bufs[flow].at[s - 1, rows_of(k)], far_bufs[flow].at[s, rows_of(k)],
            far_send.at[flow, s, k], far_recv.at[flow, s, k], block(me + (PLANE, -PLANE)[flow]),
        )

    def near(flow, k, peer=None, source=None, sent=None):
        return send(
            inputs[flow].at[rows_of(k)] if source is None else source,
            near_bufs[flow].at[rows_of(k)],
            near_send.at[flow, k] if sent is None else sent,
            near_recv.at[flow, k],
            block(me + (groups, -groups)[flow]) if peer is None else peer,
        )

    def near_detour(flow, k):
        return send(
            inputs[flow].at[rows_of(k)], near_pass, near_send.at[flow, k], pass_recv.at[0], near_stop(k)
        )

    def far_detour(flow, k):
        return send(
            inputs[flow].at[rows_of(k)], far_pass, far_send.at[flow, 0, k], pass_recv.at[1],
            (text_stop, image_stop)[flow](k),
        )

    far_special = (last, first)
    near_special = (
        jnp.logical_and(is_edge, high == 1),
        jnp.logical_and(is_edge, high == 0),
    )

    def open_special(flow):
        @pl.when(far_special[flow])
        def _():
            for k in range(CHUNKS):
                far_detour(flow, k if flow == 0 else CHUNKS - 1 - k).start()

        @pl.when(near_special[flow])
        def _():
            for k in range(CHUNKS):
                if k == (XS - 1, 0)[flow]:
                    near(flow, k).start()
                else:
                    near_detour(flow, k).start()

    def open_flows(flows):
        def open_far(k, _):
            for flow in flows:
                turns = jnp.logical_and((text_turn, image_turn)[flow], k == TURNED)

                @pl.when(jnp.logical_not(jnp.logical_or(far_special[flow], turns)))
                def _():
                    far_first(flow, k).start()

                @pl.when(turns)
                def _():
                    send(
                        inputs[flow].at[rows_of(k)], turned, far_send.at[flow, 0, k],
                        turned_sem.at[1], (text_turn_to, image_turn_to)[flow],
                    ).start()

            return 0

        for flow in flows:
            open_special(flow)
        lax.fori_loop(0, CHUNKS, open_far, 0)

    @pl.when(z > 0)
    def _():
        open_flows((0, 1))

    @pl.when(z == 0)
    def _():
        open_flows((0,))

    @pl.when(late_count > 0)
    def _():
        pl.semaphore_wait(barrier, late_count)

    @pl.when(z == 0)
    def _():
        open_flows((1,))

    loads = [
        pltpu.make_async_copy(image, own_image, load_sem.at[0]),
        pltpu.make_async_copy(text, own_text, load_sem.at[1]),
    ]
    for load in loads:
        load.start()

    pass_text = jnp.logical_and(jnp.logical_not(is_edge), high == 1)
    hands = (
        (jnp.logical_and(text_pass, jnp.logical_not(text_turn_pass)),
         far_first(0, x, text_goal, far_pass, pass_send.at[1])),
        (jnp.logical_and(image_pass, jnp.logical_not(image_turn_pass)),
         far_first(1, x, image_goal, far_pass, pass_send.at[1])),
        (text_turn_pass,
         send(far_pass, turned, pass_send.at[1], turned_sem.at[1], place(z, 0, 0, 0))),
        (image_turn_pass,
         send(far_pass, turned, pass_send.at[1], turned_sem.at[1], place(z, XS - 1, YS - 1, 1))),
        (pass_text, near(0, x, near_goal, near_pass, pass_send.at[0])),
        (low_pass, near(1, x, near_goal, near_pass, pass_send.at[0])),
    )

    for n, (mine, hand) in enumerate(hands):
        @pl.when(mine)
        def _():
            send(
                text.at[rows_of(0)], (far_pass, near_pass)[n // 4], pass_send.at[1 - n // 4],
                pass_recv.at[1 - n // 4], block(me + groups),
            ).wait_recv()
            hand.start()

    turn_step = one_if(z < HOPS) * (HOPS - z) + one_if(z >= HOPS) * (z - HOPS + 1)
    turn_cases = (
        (jnp.logical_and(z > 1, z < HOPS), send(
            turned, turned, turned_sem.at[0], turned_sem.at[1], block(me - PLANE))),
        (z == 1, send(
            turned, far_text.at[HOPS - 1, rows_of(TURNED)], turned_sem.at[0],
            far_recv.at[0, HOPS - 1, TURNED], block(me - PLANE))),
        (jnp.logical_and(z >= HOPS, z < ZS - 2), send(
            turned, turned, turned_sem.at[0], turned_sem.at[1], block(me + PLANE))),
        (z == ZS - 2, send(
            turned, far_image.at[HOPS - 1, rows_of(TURNED)], turned_sem.at[0],
            far_recv.at[1, HOPS - 1, TURNED], block(me + PLANE))),
    )

    def moved(flow, s, k):
        gone = s == ((z - HOPS), (HOPS - 1 - z))[flow]
        return jnp.logical_and(gone, k == TURNED)

    def forward(i, _):
        s, k = i // CHUNKS, lax.rem(i, CHUNKS)
        for flow in (0, 1):
            stays = jnp.logical_not(moved(flow, s, k))

            @pl.when(jnp.logical_and(stays, s == 1))
            def _():
                far_first(flow, k).wait_recv()

            @pl.when(jnp.logical_and(stays, s > 1))
            def _():
                far_next(flow, s - 1, k).wait_recv()

            @pl.when(stays)
            def _():
                far_next(flow, s, k).start()

        for mine, hand in turn_cases:
            @pl.when(jnp.logical_and(mine, jnp.logical_and(s == turn_step, k == TURNED)))
            def _():
                send(
                    text.at[rows_of(0)], turned, turned_sem.at[0], turned_sem.at[1], block(me + groups)
                ).wait_recv()
                hand.start()

        return 0

    def open_near(k, _):
        for flow in (0, 1):
            @pl.when(jnp.logical_not(near_special[flow]))
            def _():
                near(flow, k).start()

        return 0

    lax.fori_loop(CHUNKS, 2 * CHUNKS, forward, 0)
    lax.fori_loop(0, CHUNKS, open_near, 0)
    for load in loads:
        load.wait()

    scale = jnp.exp(jnp.full((1, rows), log_scale[0], jnp.float32))
    shift = bias[0]
    row_loss[...] = jnp.zeros_like(row_loss)

    def own(k, _):
        texts = own_text[rows_of(k), :]
        logits = scale * dot_nt(texts, own_image[...]) + shift
        loss, chance = halves(logits)
        line = lax.broadcasted_iota(jnp.int32, (part, rows), 0) + k * part
        positive = line == caption[...]
        loss = loss - jnp.where(positive, logits, 0.0)
        coef = (chance - positive.astype(jnp.float32)).astype(jnp.bfloat16)
        row_loss[...] += jnp.sum(loss, axis=0, keepdims=True)
        sum_text[rows_of(k), :] = jnp.dot(coef, own_image[...], preferred_element_type=jnp.float32)
        add = dot_tn(coef, texts)

        @pl.when(k == 0)
        def _():
            sum_image[...] = add

        @pl.when(k > 0)
        def _():
            sum_image[...] += add

        return 0

    lax.fori_loop(0, CHUNKS, own, 0)
    lax.fori_loop(2 * CHUNKS, HOPS * CHUNKS, forward, 0)

    def meet_text(texts):
        loss, chance = halves(scale * dot_nt(texts, own_image[...]) + shift)
        row_loss[...] += jnp.sum(loss, axis=0, keepdims=True)
        sum_image[...] += dot_tn(chance.astype(jnp.bfloat16), texts)

    def meet_image(images):
        _, chance = halves(scale * dot_nt(images, own_text[...]) + shift)
        sum_text[...] += dot_tn(chance.astype(jnp.bfloat16), images)

    def near_pair(k, _):
        near(0, k).wait_recv()
        meet_text(near_text[rows_of(k), :])
        near(1, k).wait_recv()
        meet_image(near_image[rows_of(k), :])
        return 0

    def far_pair(k, _):
        far_next(0, HOPS - 1, k).wait_recv()
        meet_text(far_text[HOPS - 1, rows_of(k), :])
        far_next(1, HOPS - 1, k).wait_recv()
        meet_image(far_image[HOPS - 1, rows_of(k), :])
        return 0

    lax.fori_loop(0, CHUNKS, near_pair, 0)
    lax.fori_loop(0, CHUNKS, far_pair, 0)
    wide = jnp.exp(jnp.full((1, image.shape[1]), log_scale[0], jnp.float32))
    grad_image[...] = (wide * sum_image[...]).astype(grad_image.dtype)
    grad_text[...] = (wide * sum_text[...]).astype(grad_text.dtype)
    loss_out[...] = (row_loss[...] / jnp.float32(3 * rows)).reshape(rows)

    def drain(k, _):
        for flow in (0, 1):
            far_first(flow, k).wait_send()
            near(flow, k).wait_send()
        return 0

    def drain_next(i, _):
        s, k = i // CHUNKS, lax.rem(i, CHUNKS)
        for flow in (0, 1):
            @pl.when(jnp.logical_not(moved(flow, s, k)))
            def _():
                far_next(flow, s, k).wait_send()

        return 0

    lax.fori_loop(0, CHUNKS, drain, 0)
    lax.fori_loop(CHUNKS, HOPS * CHUNKS, drain_next, 0)
    for mine, hand in hands + turn_cases:
        @pl.when(mine)
        def _():
            hand.wait_send()


def solution(mesh):
    groups = mesh.shape["group"]
    blocks = mesh.shape["dp"] * groups

    def body(image, text, caption, log_scale, bias):
        rows, width = image.shape
        block = pltpu.VMEM((rows, width), jnp.bfloat16)
        relayed = pltpu.VMEM((HOPS, rows, width), jnp.bfloat16)
        piece = pltpu.VMEM((rows // CHUNKS, width), jnp.bfloat16)
        total = pltpu.VMEM((rows, width), jnp.float32)
        vmem = pl.BlockSpec(memory_space=pltpu.VMEM)
        smem = pl.BlockSpec(memory_space=pltpu.SMEM)
        anywhere = pl.BlockSpec(memory_space=pl.ANY)
        grad_image, grad_text, row_loss = pl.pallas_call(
            functools.partial(kernel, groups, blocks),
            out_shape=(
                jax.ShapeDtypeStruct((rows, width), jnp.bfloat16),
                jax.ShapeDtypeStruct((rows, width), jnp.bfloat16),
                jax.ShapeDtypeStruct((rows,), jnp.float32),
            ),
            in_specs=[anywhere, anywhere, vmem, smem, smem],
            out_specs=(vmem, vmem, vmem),
            scratch_shapes=[block] * 4
            + [relayed] * 2
            + [piece] * 3
            + [total] * 2
            + [
                pltpu.VMEM((1, rows), jnp.float32),
                pltpu.SemaphoreType.DMA((2,)),
                pltpu.SemaphoreType.DMA((2, HOPS, CHUNKS)),
                pltpu.SemaphoreType.DMA((2, HOPS, CHUNKS)),
                pltpu.SemaphoreType.DMA((2, CHUNKS)),
                pltpu.SemaphoreType.DMA((2, CHUNKS)),
                pltpu.SemaphoreType.DMA((2,)),
                pltpu.SemaphoreType.DMA((2,)),
                pltpu.SemaphoreType.DMA((2,)),
            ],
            compiler_params=pltpu.CompilerParams(
                collective_id=0, has_side_effects=True, vmem_limit_bytes=54_250_000
            ),
        )(image, text, caption, log_scale.reshape(1), bias.reshape(1))
        return grad_image, grad_text, row_loss

    spec = P(("dp", "group"), None)
    return jax.shard_map(
        body,
        mesh=mesh,
        in_specs=(spec, spec, spec, P(), P()),
        out_specs=(spec, spec, P(("dp", "group"))),
        check_vma=False,
    )
```

```python
import functools

import jax
import jax.numpy as jnp
from jax import lax
from jax.experimental import pallas as pl
from jax.experimental.pallas import tpu as pltpu
from jax.sharding import PartitionSpec as P

MESH = pl.DeviceIdType.MESH
CHUNKS = 4
XS, YS, ZS = 4, 8, 12
PLANE = XS * YS * 2
HOPS = ZS // 2
TURNED = 1


def dot_nt(a, b):
    return lax.dot_general(a, b, (((1,), (1,)), ((), ())), preferred_element_type=jnp.float32)


def dot_tn(a, b):
    return lax.dot_general(a, b, (((0,), (0,)), ((), ())), preferred_element_type=jnp.float32)


def halves(logits):
    small = jnp.exp(-jnp.abs(logits))
    loss = jnp.maximum(logits, 0.0) + jnp.log1p(small)
    chance = jnp.where(logits >= 0, 1.0, small) / (1.0 + small)
    return loss, chance


def kernel(
    groups, blocks,
    image, text, caption_in, log_scale, bias,
    grad_image, grad_text, loss_out,
    own_image, own_text, near_text, near_image, far_text, far_image,
    near_pass, far_pass, turned, sum_image, sum_text, row_loss, caption,
    load_sem, far_send, far_recv, near_send, near_recv, pass_send, pass_recv, turned_sem,
):
    rows = image.shape[0]
    part = rows // CHUNKS
    me = lax.axis_index("dp") * groups + lax.axis_index("group")
    z, x, y, core = me // PLANE, lax.rem(me // (2 * YS), XS), lax.rem(me // 2, YS), lax.rem(me, 2)

    def block(at):
        at = lax.rem(at + blocks, blocks)
        return (at // groups, lax.rem(at, groups))

    def place(z, x, y, core):
        return block(((z * XS + x) * YS + y) * 2 + core)

    high = y // (YS // 2)
    edge = (XS - 1) * high
    across = 2 * high - 1
    opposite = y - across * (YS // 2)
    is_edge = x == edge
    plane_at = lax.rem(me, PLANE)
    last = plane_at == PLANE - 1
    first = plane_at == 0
    text_pass = jnp.logical_and(y == 0, core == 0)
    image_pass = jnp.logical_and(y == YS - 1, core == 1)

    near_source = place(z, edge, y, core)
    near_goal = place(z + across, XS - 1 - edge, opposite, core)

    def near_stop(q):
        return place(z, q, y, core)

    def near_sender(q):
        return place(z + across, q, opposite, core)

    text_source = place(z, XS - 1, YS - 1, 1)
    text_goal = place(z + 2, 0, 0, 0)
    image_source = place(z, 0, 0, 0)
    image_goal = place(z - 2, XS - 1, YS - 1, 1)

    def text_stop(j):
        return place(z, j, 0, 0)

    def image_stop(j):
        return place(z, j, YS - 1, 1)

    leap = PLANE + 1
    barrier = pltpu.get_barrier_semaphore()

    def one_if(condition):
        return condition.astype(jnp.int32)

    def tell(peers):
        for peer in peers:
            pl.semaphore_signal(barrier, inc=1, device_id=peer, device_id_type=MESH)

    top = z == ZS - 1
    goal_edge = jnp.logical_and(is_edge, high == 1)
    senders = [(step, block(me - step)) for step in (PLANE, groups)]
    others = [(step, block(me + step)) for step in (PLANE, groups)]

    for step, peer in senders:
        @pl.when(me >= step)
        def _():
            tell([peer])

    @pl.when(jnp.logical_and(jnp.logical_not(first), me >= leap))
    def _():
        tell([block(me - leap)])

    for step, peer in others:
        @pl.when(me + step < blocks)
        def _():
            tell([peer])

    @pl.when(jnp.logical_and(jnp.logical_not(last), me + leap < blocks))
    def _():
        tell([block(me + leap)])

    @pl.when(is_edge)
    def _():
        for n in range(1, XS):
            @pl.when(jnp.logical_not(jnp.logical_and(top, high == 1)))
            def _():
                tell([near_sender(XS - 1 - edge + across * n)])

    low_pass = jnp.logical_and(jnp.logical_not(is_edge), high == 0)

    @pl.when(jnp.logical_not(is_edge))
    def _():
        tell([near_source])

    image_senders = [place(z + 2, j, YS - 1, 1) for j in range(XS)]

    @pl.when(jnp.logical_and(last, z < ZS - 2))
    def _():
        tell(image_senders)

    @pl.when(first)
    def _():
        tell([place(z - 2, j, 0, 0) for j in range(XS)])

    @pl.when(text_pass)
    def _():
        tell([text_source])

    @pl.when(image_pass)
    def _():
        tell([image_source])

    low_mid = z == HOPS - 1
    high_mid = z == HOPS
    text_turn = jnp.logical_and(high_mid, jnp.logical_not(last))
    image_turn = jnp.logical_and(low_mid, jnp.logical_not(first))
    text_turn_pass = jnp.logical_and(jnp.logical_and(text_pass, low_mid), x == TURNED)
    image_turn_pass = jnp.logical_and(jnp.logical_and(image_pass, high_mid), x == TURNED)
    text_turn_to = block(me - PLANE + 1)
    image_turn_to = block(me + PLANE - 1)

    @pl.when(text_turn)
    def _():
        tell([text_turn_to])

    @pl.when(image_turn)
    def _():
        tell([image_turn_to])

    @pl.when(jnp.logical_and(first, low_mid))
    def _():
        tell([text_stop(TURNED)])

    @pl.when(jnp.logical_and(last, high_mid))
    def _():
        tell([image_stop(TURNED)])

    late_count = (
        one_if(z == 0) * (1 + one_if(jnp.logical_not(first)))
        + one_if(me < groups)
        + one_if(jnp.logical_and(low_pass, z == 0))
        + one_if(jnp.logical_and(image_pass, z < 2))
    )
    pl.semaphore_wait(
        barrier,
        6 - one_if(first) - one_if(last)
        + (XS - 1) * one_if(is_edge) + one_if(jnp.logical_not(is_edge))
        + XS * (one_if(last) + one_if(first))
        + one_if(text_pass) + one_if(image_pass)
        + (XS - 1) * one_if(jnp.logical_and(goal_edge, top))
        + XS * one_if(jnp.logical_and(last, z >= ZS - 2))
        + one_if(text_turn) + one_if(image_turn)
        + one_if(text_turn_pass) + one_if(image_turn_pass)
        - late_count,
    )

    for step, peer in senders:
        @pl.when(me < step)
        def _():
            tell([peer])

    @pl.when(jnp.logical_and(jnp.logical_not(first), me < leap))
    def _():
        tell([block(me - leap)])

    @pl.when(jnp.logical_and(low_pass, z == 0))
    def _():
        tell([near_goal])

    @pl.when(jnp.logical_and(image_pass, z < 2))
    def _():
        tell([image_goal])

    for step, peer in others:
        @pl.when(me + step >= blocks)
        def _():
            tell([peer])

    @pl.when(jnp.logical_and(jnp.logical_not(last), me + leap >= blocks))
    def _():
        tell([block(me + leap)])

    @pl.when(jnp.logical_and(goal_edge, top))
    def _():
        tell([near_sender(n) for n in range(1, XS)])

    @pl.when(jnp.logical_and(last, z >= ZS - 2))
    def _():
        tell(image_senders)

    def rows_of(k):
        return pl.ds(pl.multiple_of(k * part, part), part)

    def send(source, target, sent, got, peer):
        return pltpu.make_async_remote_copy(
            src_ref=source, dst_ref=target, send_sem=sent, recv_sem=got,
            device_id=peer, device_id_type=MESH,
        )

    inputs = (text, image)
    far_bufs = (far_text, far_image)
    near_bufs = (near_text, near_image)

    def far_first(flow, k, peer=None, source=None, sent=None):
        return send(
            inputs[flow].at[rows_of(k)] if source is None else source,
            far_bufs[flow].at[0, rows_of(k)],
            far_send.at[flow, 0, k] if sent is None else sent,
            far_recv.at[flow, 0, k],
            block(me + (leap, -leap)[flow]) if peer is None else peer,
        )

    def far_next(flow, s, k):
        return send(
            far_bufs[flow].at[s - 1, rows_of(k)], far_bufs[flow].at[s, rows_of(k)],
            far_send.at[flow, s, k], far_recv.at[flow, s, k], block(me + (PLANE, -PLANE)[flow]),
        )

    def near(flow, k, peer=None, source=None, sent=None):
        return send(
            inputs[flow].at[rows_of(k)] if source is None else source,
            near_bufs[flow].at[rows_of(k)],
            near_send.at[flow, k] if sent is None else sent,
            near_recv.at[flow, k],
            block(me + (groups, -groups)[flow]) if peer is None else peer,
        )

    def near_detour(flow, k):
        return send(
            inputs[flow].at[rows_of(k)], near_pass, near_send.at[flow, k], pass_recv.at[0], near_stop(k)
        )

    def far_detour(flow, k):
        return send(
            inputs[flow].at[rows_of(k)], far_pass, far_send.at[flow, 0, k], pass_recv.at[1],
            (text_stop, image_stop)[flow](k),
        )

    far_special = (last, first)
    near_special = (
        jnp.logical_and(is_edge, high == 1),
        jnp.logical_and(is_edge, high == 0),
    )

    def open_special(flow):
        @pl.when(far_special[flow])
        def _():
            for k in range(CHUNKS):
                far_detour(flow, k if flow == 0 else CHUNKS - 1 - k).start()

    def open_flows(flows):
        def open_far(k, _):
            for flow in flows:
                turns = jnp.logical_and((text_turn, image_turn)[flow], k == TURNED)

                @pl.when(jnp.logical_not(jnp.logical_or(far_special[flow], turns)))
                def _():
                    far_first(flow, k).start()

                @pl.when(turns)
                def _():
                    send(
                        inputs[flow].at[rows_of(k)], turned, far_send.at[flow, 0, k],
                        turned_sem.at[1], (text_turn_to, image_turn_to)[flow],
                    ).start()

            return 0

        for flow in flows:
            open_special(flow)
        lax.fori_loop(0, CHUNKS, open_far, 0)

    @pl.when(z > 0)
    def _():
        open_flows((0, 1))

    @pl.when(z == 0)
    def _():
        open_flows((0,))

    @pl.when(late_count > 0)
    def _():
        pl.semaphore_wait(barrier, late_count)

    @pl.when(z == 0)
    def _():
        open_flows((1,))

    loads = [
        pltpu.make_async_copy(image, own_image, load_sem.at[0]),
        pltpu.make_async_copy(text, own_text, load_sem.at[1]),
        pltpu.make_async_copy(caption_in, caption, load_sem.at[2]),
    ]
    for load in loads:
        load.start()

    pass_text = jnp.logical_and(jnp.logical_not(is_edge), high == 1)
    hands = (
        (jnp.logical_and(text_pass, jnp.logical_not(text_turn_pass)),
         far_first(0, x, text_goal, far_pass, pass_send.at[1])),
        (jnp.logical_and(image_pass, jnp.logical_not(image_turn_pass)),
         far_first(1, x, image_goal, far_pass, pass_send.at[1])),
        (text_turn_pass,
         send(far_pass, turned, pass_send.at[1], turned_sem.at[1], place(z, 0, 0, 0))),
        (image_turn_pass,
         send(far_pass, turned, pass_send.at[1], turned_sem.at[1], place(z, XS - 1, YS - 1, 1))),
        (pass_text, near(0, x, near_goal, near_pass, pass_send.at[0])),
        (low_pass, near(1, x, near_goal, near_pass, pass_send.at[0])),
    )

    def hand_on(range_of):
        for n in range_of:
            mine, hand = hands[n]

            @pl.when(mine)
            def _():
                send(
                    text.at[rows_of(0)], (far_pass, near_pass)[n // 4], pass_send.at[1 - n // 4],
                    pass_recv.at[1 - n // 4], block(me + groups),
                ).wait_recv()
                hand.start()

    hand_on(range(4))

    turn_step = one_if(z < HOPS) * (HOPS - z) + one_if(z >= HOPS) * (z - HOPS + 1)
    turn_cases = (
        (jnp.logical_and(z > 1, z < HOPS), send(
            turned, turned, turned_sem.at[0], turned_sem.at[1], block(me - PLANE))),
        (z == 1, send(
            turned, far_text.at[HOPS - 1, rows_of(TURNED)], turned_sem.at[0],
            far_recv.at[0, HOPS - 1, TURNED], block(me - PLANE))),
        (jnp.logical_and(z >= HOPS, z < ZS - 2), send(
            turned, turned, turned_sem.at[0], turned_sem.at[1], block(me + PLANE))),
        (z == ZS - 2, send(
            turned, far_image.at[HOPS - 1, rows_of(TURNED)], turned_sem.at[0],
            far_recv.at[1, HOPS - 1, TURNED], block(me + PLANE))),
    )

    def moved(flow, s, k):
        gone = s == ((z - HOPS), (HOPS - 1 - z))[flow]
        return jnp.logical_and(gone, k == TURNED)

    def forward(i, _):
        s, k = i // CHUNKS, lax.rem(i, CHUNKS)
        for flow in (0, 1):
            stays = jnp.logical_not(moved(flow, s, k))

            @pl.when(jnp.logical_and(stays, s == 1))
            def _():
                far_first(flow, k).wait_recv()

            @pl.when(jnp.logical_and(stays, s > 1))
            def _():
                far_next(flow, s - 1, k).wait_recv()

            @pl.when(stays)
            def _():
                far_next(flow, s, k).start()

        for mine, hand in turn_cases:
            @pl.when(jnp.logical_and(mine, jnp.logical_and(s == turn_step, k == TURNED)))
            def _():
                send(
                    text.at[rows_of(0)], turned, turned_sem.at[0], turned_sem.at[1], block(me + groups)
                ).wait_recv()
                hand.start()

        return 0

    def open_near(k, _):
        for flow in (0, 1):
            @pl.when(jnp.logical_not(near_special[flow]))
            def _():
                near(flow, k).start()

        return 0

    lax.fori_loop(CHUNKS, 2 * CHUNKS, forward, 0)
    for flow in (0, 1):
        @pl.when(near_special[flow])
        def _():
            for k in range(CHUNKS):
                if k == (XS - 1, 0)[flow]:
                    near(flow, k).start()
                else:
                    near_detour(flow, k).start()

    lax.fori_loop(0, CHUNKS, open_near, 0)
    for load in loads:
        load.wait()

    scale = jnp.exp(jnp.full((1, rows), log_scale[0], jnp.float32))
    shift = bias[0]
    row_loss[...] = jnp.zeros_like(row_loss)

    def own(k, _):
        texts = own_text[rows_of(k), :]
        logits = scale * dot_nt(texts, own_image[...]) + shift
        loss, chance = halves(logits)
        line = lax.broadcasted_iota(jnp.int32, (part, rows), 0) + k * part
        positive = line == caption[...]
        loss = loss - jnp.where(positive, logits, 0.0)
        coef = (chance - positive.astype(jnp.float32)).astype(jnp.bfloat16)
        row_loss[...] += jnp.sum(loss, axis=0, keepdims=True)
        sum_text[rows_of(k), :] = jnp.dot(coef, own_image[...], preferred_element_type=jnp.float32)
        add = dot_tn(coef, texts)

        @pl.when(k == 0)
        def _():
            sum_image[...] = add

        @pl.when(k > 0)
        def _():
            sum_image[...] += add

        return 0

    def own_between(k, _):
        forward(2 * CHUNKS + k, 0)
        return own(k, 0)

    lax.fori_loop(0, CHUNKS, own_between, 0)
    hand_on(range(4, len(hands)))
    lax.fori_loop(3 * CHUNKS, HOPS * CHUNKS, forward, 0)

    def meet_text(texts):
        loss, chance = halves(scale * dot_nt(texts, own_image[...]) + shift)
        row_loss[...] += jnp.sum(loss, axis=0, keepdims=True)
        sum_image[...] += dot_tn(chance.astype(jnp.bfloat16), texts)

    def meet_image(images):
        _, chance = halves(scale * dot_nt(images, own_text[...]) + shift)
        sum_text[...] += dot_tn(chance.astype(jnp.bfloat16), images)

    def near_pair(k, _):
        near(0, k).wait_recv()
        meet_text(near_text[rows_of(k), :])
        near(1, k).wait_recv()
        meet_image(near_image[rows_of(k), :])
        return 0

    def far_pair(k, _):
        far_next(0, HOPS - 1, k).wait_recv()
        meet_text(far_text[HOPS - 1, rows_of(k), :])
        far_next(1, HOPS - 1, k).wait_recv()
        meet_image(far_image[HOPS - 1, rows_of(k), :])
        return 0

    lax.fori_loop(0, CHUNKS, near_pair, 0)
    lax.fori_loop(0, CHUNKS, far_pair, 0)
    wide = jnp.exp(jnp.full((1, image.shape[1]), log_scale[0], jnp.float32))
    grad_image[...] = (wide * sum_image[...]).astype(grad_image.dtype)
    grad_text[...] = (wide * sum_text[...]).astype(grad_text.dtype)
    loss_out[...] = (row_loss[...] / jnp.float32(3 * rows)).reshape(rows)

    def drain(k, _):
        for flow in (0, 1):
            far_first(flow, k).wait_send()
            near(flow, k).wait_send()
        return 0

    def drain_next(i, _):
        s, k = i // CHUNKS, lax.rem(i, CHUNKS)
        for flow in (0, 1):
            @pl.when(jnp.logical_not(moved(flow, s, k)))
            def _():
                far_next(flow, s, k).wait_send()

        return 0

    lax.fori_loop(0, CHUNKS, drain, 0)
    lax.fori_loop(CHUNKS, HOPS * CHUNKS, drain_next, 0)
    for mine, hand in hands + turn_cases:
        @pl.when(mine)
        def _():
            hand.wait_send()


def store(*refs):
    count = len(refs) // 2
    copies = [
        pltpu.make_async_copy(refs[n], refs[count + n], refs[-1].at[n]) for n in range(count)
    ]
    for copy in copies:
        copy.start()
    for copy in copies:
        copy.wait()


def solution(mesh):
    groups = mesh.shape["group"]
    blocks = mesh.shape["dp"] * groups

    def body(image, text, caption, log_scale, bias):
        rows, width = image.shape
        block = pltpu.VMEM((rows, width), jnp.bfloat16)
        relayed = pltpu.VMEM((HOPS, rows, width), jnp.bfloat16)
        piece = pltpu.VMEM((rows // CHUNKS, width), jnp.bfloat16)
        total = pltpu.VMEM((rows, width), jnp.float32)
        vmem = pl.BlockSpec(memory_space=pltpu.VMEM)
        smem = pl.BlockSpec(memory_space=pltpu.SMEM)
        anywhere = pl.BlockSpec(memory_space=pl.ANY)
        grad_image, grad_text, row_loss = pl.pallas_call(
            functools.partial(kernel, groups, blocks),
            out_shape=(
                jax.ShapeDtypeStruct((rows, width), jnp.bfloat16),
                jax.ShapeDtypeStruct((rows, width), jnp.bfloat16),
                jax.ShapeDtypeStruct((rows,), jnp.float32),
            ),
            in_specs=[anywhere, anywhere, anywhere, smem, smem],
            out_specs=(vmem, vmem, vmem),
            scratch_shapes=[block] * 4
            + [relayed] * 2
            + [piece] * 3
            + [total] * 2
            + [
                pltpu.VMEM((1, rows), jnp.float32),
                pltpu.VMEM((1, rows), jnp.int32),
                pltpu.SemaphoreType.DMA((3,)),
                pltpu.SemaphoreType.DMA((2, HOPS, CHUNKS)),
                pltpu.SemaphoreType.DMA((2, HOPS, CHUNKS)),
                pltpu.SemaphoreType.DMA((2, CHUNKS)),
                pltpu.SemaphoreType.DMA((2, CHUNKS)),
                pltpu.SemaphoreType.DMA((2,)),
                pltpu.SemaphoreType.DMA((2,)),
                pltpu.SemaphoreType.DMA((2,)),
            ],
            compiler_params=pltpu.CompilerParams(
                collective_id=0, has_side_effects=True, vmem_limit_bytes=54_250_000
            ),
        )(image, text, caption, log_scale.reshape(1), bias.reshape(1))
        return pl.pallas_call(
            store,
            out_shape=(
                jax.ShapeDtypeStruct((rows, width), jnp.bfloat16),
                jax.ShapeDtypeStruct((rows, width), jnp.bfloat16),
                jax.ShapeDtypeStruct((rows,), jnp.float32),
            ),
            in_specs=[vmem] * 3,
            out_specs=(anywhere, anywhere, anywhere),
            scratch_shapes=[pltpu.SemaphoreType.DMA((3,))],
            compiler_params=pltpu.CompilerParams(vmem_limit_bytes=16 << 20),
        )(grad_image, grad_text, row_loss)

    spec = P(("dp", "group"), None)
    return jax.shard_map(
        body,
        mesh=mesh,
        in_specs=(spec, spec, spec, P(), P()),
        out_specs=(spec, spec, P(("dp", "group"))),
        check_vma=False,
    )
```

```python
import functools

import jax
import jax.numpy as jnp
from jax import lax
from jax.experimental import pallas as pl
from jax.experimental.pallas import tpu as pltpu
from jax.sharding import PartitionSpec as P

MESH = pl.DeviceIdType.MESH
CHUNKS = 4
XS, YS, ZS = 4, 8, 12
PLANE = XS * YS * 2
HOPS = ZS // 2
TURNED = 1


def dot_nt(a, b):
    return lax.dot_general(a, b, (((1,), (1,)), ((), ())), preferred_element_type=jnp.float32)


def dot_tn(a, b):
    return lax.dot_general(a, b, (((0,), (0,)), ((), ())), preferred_element_type=jnp.float32)


def halves(logits):
    small = jnp.exp(-jnp.abs(logits))
    loss = jnp.maximum(logits, 0.0) + jnp.log1p(small)
    chance = jnp.where(logits >= 0, 1.0, small) / (1.0 + small)
    return loss, chance


def kernel(
    groups, blocks,
    image, text, caption_in, log_scale, bias,
    grad_image, grad_text, loss_out,
    own_image, own_text, near_text, near_image, far_text, far_image,
    near_pass, far_pass, turned, sum_image, sum_text, row_loss, caption,
    load_sem, far_send, far_recv, near_send, near_recv, pass_send, pass_recv, turned_sem,
):
    rows = image.shape[0]
    part = rows // CHUNKS
    me = lax.axis_index("dp") * groups + lax.axis_index("group")
    z, x, y, core = me // PLANE, lax.rem(me // (2 * YS), XS), lax.rem(me // 2, YS), lax.rem(me, 2)

    def block(at):
        at = lax.rem(at + blocks, blocks)
        return (at // groups, lax.rem(at, groups))

    def place(z, x, y, core):
        return block(((z * XS + x) * YS + y) * 2 + core)

    high = y // (YS // 2)
    edge = (XS - 1) * high
    across = 2 * high - 1
    opposite = y - across * (YS // 2)
    is_edge = x == edge
    plane_at = lax.rem(me, PLANE)
    last = plane_at == PLANE - 1
    first = plane_at == 0
    text_pass = jnp.logical_and(y == 0, core == 0)
    image_pass = jnp.logical_and(y == YS - 1, core == 1)

    near_source = place(z, edge, y, core)
    near_goal = place(z + across, XS - 1 - edge, opposite, core)

    def near_stop(q):
        return place(z, q, y, core)

    def near_sender(q):
        return place(z + across, q, opposite, core)

    text_source = place(z, XS - 1, YS - 1, 1)
    text_goal = place(z + 2, 0, 0, 0)
    image_source = place(z, 0, 0, 0)
    image_goal = place(z - 2, XS - 1, YS - 1, 1)

    def text_stop(j):
        return place(z, j, 0, 0)

    def image_stop(j):
        return place(z, j, YS - 1, 1)

    leap = PLANE + 1
    barrier = pltpu.get_barrier_semaphore()

    def one_if(condition):
        return condition.astype(jnp.int32)

    def tell(peers):
        for peer in peers:
            pl.semaphore_signal(barrier, inc=1, device_id=peer, device_id_type=MESH)

    top = z == ZS - 1
    goal_edge = jnp.logical_and(is_edge, high == 1)
    senders = [(step, block(me - step)) for step in (PLANE, groups)]
    others = [(step, block(me + step)) for step in (PLANE, groups)]

    for step, peer in senders:
        @pl.when(me >= step)
        def _():
            tell([peer])

    @pl.when(jnp.logical_and(jnp.logical_not(first), me >= leap))
    def _():
        tell([block(me - leap)])

    for step, peer in others:
        @pl.when(me + step < blocks)
        def _():
            tell([peer])

    @pl.when(jnp.logical_and(jnp.logical_not(last), me + leap < blocks))
    def _():
        tell([block(me + leap)])

    @pl.when(is_edge)
    def _():
        for n in range(1, XS):
            @pl.when(jnp.logical_not(jnp.logical_and(top, high == 1)))
            def _():
                tell([near_sender(XS - 1 - edge + across * n)])

    low_pass = jnp.logical_and(jnp.logical_not(is_edge), high == 0)

    @pl.when(jnp.logical_not(is_edge))
    def _():
        tell([near_source])

    image_senders = [place(z + 2, j, YS - 1, 1) for j in range(XS)]

    @pl.when(jnp.logical_and(last, z < ZS - 2))
    def _():
        tell(image_senders)

    @pl.when(first)
    def _():
        tell([place(z - 2, j, 0, 0) for j in range(XS)])

    @pl.when(text_pass)
    def _():
        tell([text_source])

    @pl.when(image_pass)
    def _():
        tell([image_source])

    low_mid = z == HOPS - 1
    high_mid = z == HOPS
    text_turn = jnp.logical_and(high_mid, jnp.logical_not(last))
    image_turn = jnp.logical_and(low_mid, jnp.logical_not(first))
    text_turn_pass = jnp.logical_and(jnp.logical_and(text_pass, low_mid), x == TURNED)
    image_turn_pass = jnp.logical_and(jnp.logical_and(image_pass, high_mid), x == TURNED)
    text_turn_to = block(me - PLANE + 1)
    image_turn_to = block(me + PLANE - 1)

    @pl.when(text_turn)
    def _():
        tell([text_turn_to])

    @pl.when(image_turn)
    def _():
        tell([image_turn_to])

    @pl.when(jnp.logical_and(first, low_mid))
    def _():
        tell([text_stop(TURNED)])

    @pl.when(jnp.logical_and(last, high_mid))
    def _():
        tell([image_stop(TURNED)])

    late_count = (
        one_if(z == 0) * (1 + one_if(jnp.logical_not(first)))
        + one_if(me < groups)
        + one_if(jnp.logical_and(low_pass, z == 0))
        + one_if(jnp.logical_and(image_pass, z < 2))
    )
    pl.semaphore_wait(
        barrier,
        6 - one_if(first) - one_if(last)
        + (XS - 1) * one_if(is_edge) + one_if(jnp.logical_not(is_edge))
        + XS * (one_if(last) + one_if(first))
        + one_if(text_pass) + one_if(image_pass)
        + (XS - 1) * one_if(jnp.logical_and(goal_edge, top))
        + XS * one_if(jnp.logical_and(last, z >= ZS - 2))
        + one_if(text_turn) + one_if(image_turn)
        + one_if(text_turn_pass) + one_if(image_turn_pass)
        - late_count,
    )

    for step, peer in senders:
        @pl.when(me < step)
        def _():
            tell([peer])

    @pl.when(jnp.logical_and(jnp.logical_not(first), me < leap))
    def _():
        tell([block(me - leap)])

    @pl.when(jnp.logical_and(low_pass, z == 0))
    def _():
        tell([near_goal])

    @pl.when(jnp.logical_and(image_pass, z < 2))
    def _():
        tell([image_goal])

    for step, peer in others:
        @pl.when(me + step >= blocks)
        def _():
            tell([peer])

    @pl.when(jnp.logical_and(jnp.logical_not(last), me + leap >= blocks))
    def _():
        tell([block(me + leap)])

    @pl.when(jnp.logical_and(goal_edge, top))
    def _():
        tell([near_sender(n) for n in range(1, XS)])

    @pl.when(jnp.logical_and(last, z >= ZS - 2))
    def _():
        tell(image_senders)

    def rows_of(k):
        return pl.ds(pl.multiple_of(k * part, part), part)

    def send(source, target, sent, got, peer):
        return pltpu.make_async_remote_copy(
            src_ref=source, dst_ref=target, send_sem=sent, recv_sem=got,
            device_id=peer, device_id_type=MESH,
        )

    inputs = (text, image)
    far_bufs = (far_text, far_image)
    near_bufs = (near_text, near_image)

    def far_first(flow, k, peer=None, source=None, sent=None):
        return send(
            inputs[flow].at[rows_of(k)] if source is None else source,
            far_bufs[flow].at[0, rows_of(k)],
            far_send.at[flow, 0, k] if sent is None else sent,
            far_recv.at[flow, 0, k],
            block(me + (leap, -leap)[flow]) if peer is None else peer,
        )

    def far_next(flow, s, k):
        return send(
            far_bufs[flow].at[s - 1, rows_of(k)], far_bufs[flow].at[s, rows_of(k)],
            far_send.at[flow, s, k], far_recv.at[flow, s, k], block(me + (PLANE, -PLANE)[flow]),
        )

    def near(flow, k, peer=None, source=None, sent=None):
        return send(
            inputs[flow].at[rows_of(k)] if source is None else source,
            near_bufs[flow].at[rows_of(k)],
            near_send.at[flow, k] if sent is None else sent,
            near_recv.at[flow, k],
            block(me + (groups, -groups)[flow]) if peer is None else peer,
        )

    def near_detour(flow, k):
        return send(
            inputs[flow].at[rows_of(k)], near_pass, near_send.at[flow, k], pass_recv.at[0], near_stop(k)
        )

    def far_detour(flow, k):
        return send(
            inputs[flow].at[rows_of(k)], far_pass, far_send.at[flow, 0, k], pass_recv.at[1],
            (text_stop, image_stop)[flow](k),
        )

    far_special = (last, first)
    near_special = (
        jnp.logical_and(is_edge, high == 1),
        jnp.logical_and(is_edge, high == 0),
    )

    def open_special(flow):
        @pl.when(far_special[flow])
        def _():
            for k in range(CHUNKS):
                far_detour(flow, k if flow == 0 else CHUNKS - 1 - k).start()

    def open_flows(flows):
        def open_far(k, _):
            for flow in flows:
                turns = jnp.logical_and((text_turn, image_turn)[flow], k == TURNED)

                @pl.when(jnp.logical_not(jnp.logical_or(far_special[flow], turns)))
                def _():
                    far_first(flow, k).start()

                @pl.when(turns)
                def _():
                    send(
                        inputs[flow].at[rows_of(k)], turned, far_send.at[flow, 0, k],
                        turned_sem.at[1], (text_turn_to, image_turn_to)[flow],
                    ).start()

            return 0

        for flow in flows:
            open_special(flow)
        lax.fori_loop(0, CHUNKS, open_far, 0)

    @pl.when(z > 0)
    def _():
        open_flows((0, 1))

    @pl.when(z == 0)
    def _():
        open_flows((0,))

    @pl.when(late_count > 0)
    def _():
        pl.semaphore_wait(barrier, late_count)

    @pl.when(z == 0)
    def _():
        open_flows((1,))

    loads = [
        pltpu.make_async_copy(image, own_image, load_sem.at[0]),
        pltpu.make_async_copy(text, own_text, load_sem.at[1]),
        pltpu.make_async_copy(caption_in, caption, load_sem.at[2]),
    ]
    for load in loads:
        load.start()

    pass_text = jnp.logical_and(jnp.logical_not(is_edge), high == 1)
    hands = (
        (jnp.logical_and(text_pass, jnp.logical_not(text_turn_pass)),
         far_first(0, x, text_goal, far_pass, pass_send.at[1])),
        (jnp.logical_and(image_pass, jnp.logical_not(image_turn_pass)),
         far_first(1, x, image_goal, far_pass, pass_send.at[1])),
        (text_turn_pass,
         send(far_pass, turned, pass_send.at[1], turned_sem.at[1], place(z, 0, 0, 0))),
        (image_turn_pass,
         send(far_pass, turned, pass_send.at[1], turned_sem.at[1], place(z, XS - 1, YS - 1, 1))),
        (pass_text, near(0, x, near_goal, near_pass, pass_send.at[0])),
        (low_pass, near(1, x, near_goal, near_pass, pass_send.at[0])),
    )

    def hand_on(range_of):
        for n in range_of:
            mine, hand = hands[n]

            @pl.when(mine)
            def _():
                send(
                    text.at[rows_of(0)], (far_pass, near_pass)[n // 4], pass_send.at[1 - n // 4],
                    pass_recv.at[1 - n // 4], block(me + groups),
                ).wait_recv()
                hand.start()

    hand_on(range(4))

    turn_step = one_if(z < HOPS) * (HOPS - z) + one_if(z >= HOPS) * (z - HOPS + 1)
    turn_cases = (
        (jnp.logical_and(z > 1, z < HOPS), send(
            turned, turned, turned_sem.at[0], turned_sem.at[1], block(me - PLANE))),
        (z == 1, send(
            turned, far_text.at[HOPS - 1, rows_of(TURNED)], turned_sem.at[0],
            far_recv.at[0, HOPS - 1, TURNED], block(me - PLANE))),
        (jnp.logical_and(z >= HOPS, z < ZS - 2), send(
            turned, turned, turned_sem.at[0], turned_sem.at[1], block(me + PLANE))),
        (z == ZS - 2, send(
            turned, far_image.at[HOPS - 1, rows_of(TURNED)], turned_sem.at[0],
            far_recv.at[1, HOPS - 1, TURNED], block(me + PLANE))),
    )

    def moved(flow, s, k):
        gone = s == ((z - HOPS), (HOPS - 1 - z))[flow]
        return jnp.logical_and(gone, k == TURNED)

    def forward(i, _):
        s, k = i // CHUNKS, lax.rem(i, CHUNKS)
        for flow in (0, 1):
            stays = jnp.logical_not(moved(flow, s, k))

            @pl.when(jnp.logical_and(stays, s == 1))
            def _():
                far_first(flow, k).wait_recv()

            @pl.when(jnp.logical_and(stays, s > 1))
            def _():
                far_next(flow, s - 1, k).wait_recv()

            @pl.when(stays)
            def _():
                far_next(flow, s, k).start()

        for mine, hand in turn_cases:
            @pl.when(jnp.logical_and(mine, jnp.logical_and(s == turn_step, k == TURNED)))
            def _():
                send(
                    text.at[rows_of(0)], turned, turned_sem.at[0], turned_sem.at[1], block(me + groups)
                ).wait_recv()
                hand.start()

        return 0

    def open_near(k, _):
        for flow in (0, 1):
            @pl.when(jnp.logical_not(near_special[flow]))
            def _():
                near(flow, k).start()

        return 0

    lax.fori_loop(CHUNKS, 2 * CHUNKS, forward, 0)
    for flow in (0, 1):
        @pl.when(near_special[flow])
        def _():
            for k in range(CHUNKS):
                if k == (XS - 1, 0)[flow]:
                    near(flow, k).start()
                else:
                    near_detour(flow, k).start()

    lax.fori_loop(0, CHUNKS, open_near, 0)
    for load in loads:
        load.wait()

    scale = jnp.exp(jnp.full((1, rows), log_scale[0], jnp.float32))
    shift = bias[0]
    row_loss[...] = jnp.zeros_like(row_loss)

    def own(k, _):
        texts = own_text[rows_of(k), :]
        logits = scale * dot_nt(texts, own_image[...]) + shift
        loss, chance = halves(logits)
        line = lax.broadcasted_iota(jnp.int32, (part, rows), 0) + k * part
        positive = line == caption[...]
        loss = loss - jnp.where(positive, logits, 0.0)
        coef = (chance - positive.astype(jnp.float32)).astype(jnp.bfloat16)
        row_loss[...] += jnp.sum(loss, axis=0, keepdims=True)
        sum_text[rows_of(k), :] = jnp.dot(coef, own_image[...], preferred_element_type=jnp.float32)
        add = dot_tn(coef, texts)

        @pl.when(k == 0)
        def _():
            sum_image[...] = add

        @pl.when(k > 0)
        def _():
            sum_image[...] += add

        return 0

    def own_between(k, _):
        forward(2 * CHUNKS + k, 0)
        return own(k, 0)

    lax.fori_loop(0, CHUNKS, own_between, 0)
    hand_on(range(4, len(hands)))
    lax.fori_loop(3 * CHUNKS, HOPS * CHUNKS, forward, 0)

    def meet_text(texts):
        loss, chance = halves(scale * dot_nt(texts, own_image[...]) + shift)
        row_loss[...] += jnp.sum(loss, axis=0, keepdims=True)
        sum_image[...] += dot_tn(chance.astype(jnp.bfloat16), texts)

    def meet_image(images):
        _, chance = halves(scale * dot_nt(images, own_text[...]) + shift)
        sum_text[...] += dot_tn(chance.astype(jnp.bfloat16), images)

    def near_pair(k, _):
        near(0, k).wait_recv()
        meet_text(near_text[rows_of(k), :])
        near(1, k).wait_recv()
        meet_image(near_image[rows_of(k), :])
        return 0

    def far_pair(k, _):
        far_next(0, HOPS - 1, k).wait_recv()
        meet_text(far_text[HOPS - 1, rows_of(k), :])
        far_next(1, HOPS - 1, k).wait_recv()
        meet_image(far_image[HOPS - 1, rows_of(k), :])
        return 0

    lax.fori_loop(0, CHUNKS, near_pair, 0)
    def drain(k, _):
        for flow in (0, 1):
            far_first(flow, k).wait_send()
            near(flow, k).wait_send()
        return 0

    def drain_next(i, _):
        s, k = i // CHUNKS, lax.rem(i, CHUNKS)
        for flow in (0, 1):
            @pl.when(jnp.logical_not(moved(flow, s, k)))
            def _():
                far_next(flow, s, k).wait_send()

        return 0

    lax.fori_loop(0, CHUNKS, drain, 0)
    lax.fori_loop(CHUNKS, (HOPS - 1) * CHUNKS, drain_next, 0)
    lax.fori_loop(0, CHUNKS, far_pair, 0)
    wide = jnp.exp(jnp.full((1, image.shape[1]), log_scale[0], jnp.float32))
    grad_image[...] = (wide * sum_image[...]).astype(grad_image.dtype)
    grad_text[...] = (wide * sum_text[...]).astype(grad_text.dtype)
    loss_out[...] = (row_loss[...] / jnp.float32(3 * rows)).reshape(rows)

    lax.fori_loop((HOPS - 1) * CHUNKS, HOPS * CHUNKS, drain_next, 0)
    for mine, hand in hands + turn_cases:
        @pl.when(mine)
        def _():
            hand.wait_send()


def store(*refs):
    count = len(refs) // 2
    copies = [
        pltpu.make_async_copy(refs[n], refs[count + n], refs[-1].at[n]) for n in range(count)
    ]
    for copy in copies:
        copy.start()
    for copy in copies:
        copy.wait()


def solution(mesh):
    groups = mesh.shape["group"]
    blocks = mesh.shape["dp"] * groups

    def body(image, text, caption, log_scale, bias):
        rows, width = image.shape
        block = pltpu.VMEM((rows, width), jnp.bfloat16)
        relayed = pltpu.VMEM((HOPS, rows, width), jnp.bfloat16)
        piece = pltpu.VMEM((rows // CHUNKS, width), jnp.bfloat16)
        total = pltpu.VMEM((rows, width), jnp.float32)
        vmem = pl.BlockSpec(memory_space=pltpu.VMEM)
        smem = pl.BlockSpec(memory_space=pltpu.SMEM)
        anywhere = pl.BlockSpec(memory_space=pl.ANY)
        grad_image, grad_text, row_loss = pl.pallas_call(
            functools.partial(kernel, groups, blocks),
            out_shape=(
                jax.ShapeDtypeStruct((rows, width), jnp.bfloat16),
                jax.ShapeDtypeStruct((rows, width), jnp.bfloat16),
                jax.ShapeDtypeStruct((rows,), jnp.float32),
            ),
            in_specs=[anywhere, anywhere, anywhere, smem, smem],
            out_specs=(vmem, vmem, vmem),
            scratch_shapes=[block] * 4
            + [relayed] * 2
            + [piece] * 3
            + [total] * 2
            + [
                pltpu.VMEM((1, rows), jnp.float32),
                pltpu.VMEM((1, rows), jnp.int32),
                pltpu.SemaphoreType.DMA((3,)),
                pltpu.SemaphoreType.DMA((2, HOPS, CHUNKS)),
                pltpu.SemaphoreType.DMA((2, HOPS, CHUNKS)),
                pltpu.SemaphoreType.DMA((2, CHUNKS)),
                pltpu.SemaphoreType.DMA((2, CHUNKS)),
                pltpu.SemaphoreType.DMA((2,)),
                pltpu.SemaphoreType.DMA((2,)),
                pltpu.SemaphoreType.DMA((2,)),
            ],
            compiler_params=pltpu.CompilerParams(
                collective_id=0, has_side_effects=True, vmem_limit_bytes=54_250_000
            ),
        )(image, text, caption, log_scale.reshape(1), bias.reshape(1))
        return pl.pallas_call(
            store,
            out_shape=(
                jax.ShapeDtypeStruct((rows, width), jnp.bfloat16),
                jax.ShapeDtypeStruct((rows, width), jnp.bfloat16),
                jax.ShapeDtypeStruct((rows,), jnp.float32),
            ),
            in_specs=[vmem] * 3,
            out_specs=(anywhere, anywhere, anywhere),
            scratch_shapes=[pltpu.SemaphoreType.DMA((3,))],
            compiler_params=pltpu.CompilerParams(vmem_limit_bytes=16 << 20),
        )(grad_image, grad_text, row_loss)

    spec = P(("dp", "group"), None)
    return jax.shard_map(
        body,
        mesh=mesh,
        in_specs=(spec, spec, spec, P(), P()),
        out_specs=(spec, spec, P(("dp", "group"))),
        check_vma=False,
    )
```
